32 devices in a mesh: dp: 4 (over y, core), fsdp: 8 (over z, x).
Axes of the slice: x: 2, y: 2, z: 4, core: 2. Of those that a mesh axis runs over, the one named last changes fastest.
Arguments:
- small_images: bfloat16 [64, 196, 256], P(('dp', 'fsdp')), may hold values from -6 to 6
- large_images: bfloat16 [256, 784, 256], P(('dp', 'fsdp')), may hold values from -6 to 6
- small_cot: bfloat16 [64, 196, 256], P(('dp', 'fsdp'))
- large_cot: bfloat16 [256, 784, 256], P(('dp', 'fsdp'))
- counts: int32 [32, 2], P(('dp', 'fsdp')), may hold values from 0 to 8, as said below
- qkv_master: float32 [256, 768], P(('dp', 'fsdp')), may hold values from -0.25 to 0.25
- qkv_first: float32 [256, 768], P(('dp', 'fsdp')), may hold values from -0.015625 to 0.015625
- qkv_second: float32 [256, 768], P(('dp', 'fsdp')), may hold values from 1.2715658e-06 to 5.086263e-06
- proj_master: float32 [256, 256], P(None, ('dp', 'fsdp')), may hold values from -0.75 to 0.75
- proj_first: float32 [256, 256], P(None, ('dp', 'fsdp')), may hold values from -0.015625 to 0.015625
- proj_second: float32 [256, 256], P(None, ('dp', 'fsdp')), may hold values from 1.2715658e-06 to 5.086263e-06
- fc1_master: float32 [256, 1024], P(('dp', 'fsdp')), may hold values from -0.375 to 0.375
- fc1_first: float32 [256, 1024], P(('dp', 'fsdp')), may hold values from -0.015625 to 0.015625
- fc1_second: float32 [256, 1024], P(('dp', 'fsdp')), may hold values from 1.2715658e-06 to 5.086263e-06
- fc2_master: float32 [1024, 256], P(None, ('dp', 'fsdp')), may hold values from -0.1875 to 0.1875
- fc2_first: float32 [1024, 256], P(None, ('dp', 'fsdp')), may hold values from -0.015625 to 0.015625
- fc2_second: float32 [1024, 256], P(None, ('dp', 'fsdp')), may hold values from 1.2715658e-06 to 5.086263e-06
- vec_master: float32 [22, 256], P(None, ('dp', 'fsdp'))
- vec_first: float32 [22, 256], P(None, ('dp', 'fsdp')), may hold values from -0.015625 to 0.015625
- vec_second: float32 [22, 256], P(None, ('dp', 'fsdp')), may hold values from 1.2715658e-06 to 5.086263e-06
Outputs:
- small_output: bfloat16 [64, 196, 256], P(('dp', 'fsdp'))
- large_output: bfloat16 [256, 784, 256], P(('dp', 'fsdp'))
- small_input_grad: float32 [64, 196, 256], P(('dp', 'fsdp'))
- large_input_grad: float32 [256, 784, 256], P(('dp', 'fsdp'))
- qkv_new: float32 [256, 768], P(('dp', 'fsdp'))
- qkv_first_new: float32 [256, 768], P(('dp', 'fsdp'))
- qkv_second_new: float32 [256, 768], P(('dp', 'fsdp'))
- qkv_copy: bfloat16 [256, 768], P(('dp', 'fsdp'))
- proj_new: float32 [256, 256], P(None, ('dp', 'fsdp'))
- proj_first_new: float32 [256, 256], P(None, ('dp', 'fsdp'))
- proj_second_new: float32 [256, 256], P(None, ('dp', 'fsdp'))
- proj_copy: bfloat16 [256, 256], P(None, ('dp', 'fsdp'))
- fc1_new: float32 [256, 1024], P(('dp', 'fsdp'))
- fc1_first_new: float32 [256, 1024], P(('dp', 'fsdp'))
- fc1_second_new: float32 [256, 1024], P(('dp', 'fsdp'))
- fc1_copy: bfloat16 [256, 1024], P(('dp', 'fsdp'))
- fc2_new: float32 [1024, 256], P(None, ('dp', 'fsdp'))
- fc2_first_new: float32 [1024, 256], P(None, ('dp', 'fsdp'))
- fc2_second_new: float32 [1024, 256], P(None, ('dp', 'fsdp'))
- fc2_copy: bfloat16 [1024, 256], P(None, ('dp', 'fsdp'))
- vec_new: float32 [22, 256], P(None, ('dp', 'fsdp'))
- vec_first_new: float32 [22, 256], P(None, ('dp', 'fsdp'))
- vec_second_new: float32 [22, 256], P(None, ('dp', 'fsdp'))
- vec_copy: bfloat16 [22, 256], P(None, ('dp', 'fsdp'))
- grad_norm: float32 [], replicated
The draws below stay inside these ranges and needn't reach their ends.
Inputs may be any that keep to these rules, and one draw needn't show every extreme that they name: counts[d, 0] and counts[d, 1] are the live image slots of the first and second bucket on device d (devices in the order dp, then fsdp); the slots below the count are live. The first is at most 2 and equals it on some device, the second at most 8 and equals it on some device.
All inputs are finite; a program needn't handle non-finite values.
Results may differ from the reference program's by a relative error of at most 0.008.
The reference program's roundings to bfloat16 on the way count: a program that leaves them out, or rounds other values in their place, can miss the bound.
Values may be sent and summed in bfloat16 or wider, within the bound.
No kernel may reach another device: no remote copies, remote signals or barrier semaphores. Data moves between devices by JAX's collectives and lax.ppermute only.
A program may use at most 448 MiB of HBM per device.

```python
import math
import jax
import jax.numpy as jnp
from jax import lax

D = 256
FF = 1024
HEADS = 8
STRIPE = 7
SIDE_A = 14
SIDE_B = 28
CA = 2
CB = 8
STEP = 10
NV = 22
SMALL_IMAGES = 64
LARGE_IMAGES = 256
N_DP = 4
N_FSDP = 8
DEVICES = 32


def rising(column_count, spread):
    device_place = jnp.arange(column_count) // (column_count // DEVICES)
    inner_frac = (device_place % N_FSDP).astype(jnp.float32) / max(N_FSDP - 1, 1)
    outer_frac = (device_place // N_FSDP).astype(jnp.float32) / max(N_DP - 1, 1)
    return (1.0 + spread * inner_frac) * (1.0 + spread * outer_frac)


def draw_small_cot(key, part):
    key = jax.random.fold_in(key, 11)
    shape_all = (SMALL_IMAGES, SIDE_A * SIDE_A, D)
    values = jax.random.normal(key, shape_all, jnp.float32) * rising(D, 0.73)
    return values.astype(jnp.bfloat16)


def draw_large_cot(key, part):
    key = jax.random.fold_in(key, 12)
    shape_all = (LARGE_IMAGES, SIDE_B * SIDE_B, D)
    values = jax.random.normal(key, shape_all, jnp.float32) * rising(D, 0.73)
    return values.astype(jnp.bfloat16)


def draw_counts(key, part):
    key = jax.random.fold_in(key, 13)
    first_key, second_key, pick_key = jax.random.split(key, 3)
    small_live = jax.random.randint(first_key, (DEVICES,), 0, CA + 1)
    large_live = jax.random.randint(second_key, (DEVICES,), 0, CB + 1)
    chosen = jax.random.randint(pick_key, (2,), 0, DEVICES)
    device_rows = jnp.arange(DEVICES)
    small_live = jnp.where(device_rows == chosen[0], CA, small_live)
    large_live = jnp.where(device_rows == chosen[1], CB, large_live)
    return jnp.stack([small_live, large_live], axis=1).astype(jnp.int32)


def draw_vec_master(key, part):
    key = jax.random.fold_in(key, 17)
    row_index = jnp.arange(NV)[:, None]
    gain_rows = (row_index == 0) | (row_index == 5)
    noise_values = jax.random.normal(key, (NV, D), jnp.float32)
    gains = rising(D, 0.73)[None, :] * (1.0 + 0.1 * noise_values)
    return jnp.where(gain_rows, gains, 0.3 * noise_values).astype(jnp.float32)


def shard_levels(own_key, dims, shards, smallest, high):
    loudness, own = 1.0, jax.random.fold_in(own_key, 6)
    for dim, shards_of in shards:
        steps = jnp.exp(jax.random.uniform(jax.random.fold_in(own, dim), (shards_of,), jnp.float32, smallest / len(shards), high / len(shards)))
        loudness = loudness * jnp.repeat(steps, dims[dim] // shards_of).reshape([-1 if axis == dim else 1 for axis in range(len(dims))])
    return loudness


def scatter_about(stream_key, dims, deviation, limit, shards=(), held_as=jnp.bfloat16):
    factor_of = shard_levels(stream_key, dims, shards, -0.22, 0.18) if shards else 1.0
    values = jax.random.normal(stream_key, dims, jnp.float32) * deviation * factor_of
    return jnp.minimum(jnp.maximum(values, -limit), limit).astype(held_as)


def setup_inputs(seed: int = 0) -> dict:
    keys = jax.random.split(jax.random.key(seed), 21)
    small_images = scatter_about(keys[0], (SMALL_IMAGES, SIDE_A * SIDE_A, D), 1.0, 6.0, ((0, 32),))
    large_images = scatter_about(keys[1], (LARGE_IMAGES, SIDE_B * SIDE_B, D), 1.0, 6.0, ((0, 32),))
    small_cot = draw_small_cot(jax.random.fold_in(keys[20], 71), 0)
    large_cot = draw_large_cot(jax.random.fold_in(keys[20], 71), 0)
    counts = draw_counts(jax.random.fold_in(keys[20], 71), 0)
    qkv_master = scatter_about(keys[5], (D, 3 * D), (2 * D) ** -0.5, 0.25, ((0, 32),), jnp.float32)
    qkv_first = scatter_about(keys[6], (D, 3 * D), ((4 * D * D + 2 * D * FF) ** -0.5), 0.015625, ((0, 32),), jnp.float32)
    qkv_second = jnp.clip(jnp.exp(math.log(5.086263172415784e-06) - 1.3862944 * jax.random.uniform(keys[7], (D, 3 * D), jnp.float32) ** shard_levels(keys[7], (D, 3 * D), ((0, 32),), -0.2, 0.2)), 1.271565793103946e-06, 5.086263172415784e-06)
    proj_master = scatter_about(keys[8], (D, D), (D // 4) ** -0.5, 0.75, ((1, 32),), jnp.float32)
    proj_first = scatter_about(keys[9], (D, D), ((4 * D * D + 2 * D * FF) ** -0.5), 0.015625, ((1, 32),), jnp.float32)
    proj_second = jnp.clip(jnp.exp(math.log(5.086263172415784e-06) - 1.3862944 * jax.random.uniform(keys[10], (D, D), jnp.float32) ** shard_levels(keys[10], (D, D), ((1, 32),), -0.2, 0.2)), 1.271565793103946e-06, 5.086263172415784e-06)
    fc1_master = scatter_about(keys[11], (D, FF), D ** -0.5, 0.375, ((0, 32),), jnp.float32)
    fc1_first = scatter_about(keys[12], (D, FF), ((4 * D * D + 2 * D * FF) ** -0.5), 0.015625, ((0, 32),), jnp.float32)
    fc1_second = jnp.clip(jnp.exp(math.log(5.086263172415784e-06) - 1.3862944 * jax.random.uniform(keys[13], (D, FF), jnp.float32) ** shard_levels(keys[13], (D, FF), ((0, 32),), -0.2, 0.2)), 1.271565793103946e-06, 5.086263172415784e-06)
    fc2_master = scatter_about(keys[14], (FF, D), FF ** -0.5, 0.1875, ((1, 32),), jnp.float32)
    fc2_first = scatter_about(keys[15], (FF, D), ((4 * D * D + 2 * D * FF) ** -0.5), 0.015625, ((1, 32),), jnp.float32)
    fc2_second = jnp.clip(jnp.exp(math.log(5.086263172415784e-06) - 1.3862944 * jax.random.uniform(keys[16], (FF, D), jnp.float32) ** shard_levels(keys[16], (FF, D), ((1, 32),), -0.2, 0.2)), 1.271565793103946e-06, 5.086263172415784e-06)
    vec_master = draw_vec_master(jax.random.fold_in(keys[20], 71), 0)
    vec_first = scatter_about(keys[18], (NV, D), ((4 * D * D + 2 * D * FF) ** -0.5), 0.015625, ((1, 32),), jnp.float32)
    vec_second = jnp.clip(jnp.exp(math.log(5.086263172415784e-06) - 1.3862944 * jax.random.uniform(keys[19], (NV, D), jnp.float32) ** shard_levels(keys[19], (NV, D), ((1, 32),), -0.2, 0.2)), 1.271565793103946e-06, 5.086263172415784e-06)
    return dict(small_images=small_images, large_images=large_images, small_cot=small_cot, large_cot=large_cot, counts=counts, qkv_master=qkv_master, qkv_first=qkv_first, qkv_second=qkv_second, proj_master=proj_master, proj_first=proj_first, proj_second=proj_second, fc1_master=fc1_master, fc1_first=fc1_first, fc1_second=fc1_second, fc2_master=fc2_master, fc2_first=fc2_first, fc2_second=fc2_second, vec_master=vec_master, vec_first=vec_first, vec_second=vec_second)


@jax.custom_vjp
def low(v):
    return lax.optimization_barrier(v.astype(jnp.bfloat16)).astype(jnp.float32)

@jax.custom_vjp
def low_back(v):
    return v

def low_keep(v):
    return (low(v), None)

def low_pass(kept, grad):
    return (grad,)

def back_keep(v):
    return (v, None)

def back_low(kept, grad):
    return (low(grad),)
low.defvjp(low_keep, low_pass)
low_back.defvjp(back_keep, back_low)
epsilon = 1e-05
clip_norm = 1.0
beta_one = 0.5
beta_two = 0.5
rate_matrix = 0.1
rate_vector = 0.5
decay_matrix = 0.05
adam_epsilon = 1e-08

def matmul_high(left, right):
    return jnp.einsum('...d,de->...e', left, right, precision=lax.Precision.HIGHEST)

def layer_norm(values, gain_row, shift_row):
    centered = values - lax.optimization_barrier(jnp.mean(values, axis=-1, keepdims=True))
    variance = lax.optimization_barrier(jnp.mean(centered * centered, axis=-1, keepdims=True))
    return centered * lax.rsqrt(variance + epsilon) * gain_row + shift_row

def to_stripes(values, grid_side, vertical):
    image_count, model_width = (values.shape[0], values.shape[-1])
    if vertical:
        image_grid = values.reshape(image_count, grid_side, grid_side // STRIPE, STRIPE, model_width)
        image_grid = jnp.transpose(image_grid, (0, 2, 1, 3, 4))
        return image_grid.reshape(image_count * (grid_side // STRIPE), grid_side * STRIPE, model_width)
    return values.reshape(image_count * (grid_side // STRIPE), grid_side * STRIPE, model_width)

def from_stripes(values, image_count, grid_side, vertical):
    model_width = values.shape[-1]
    if vertical:
        image_grid = values.reshape(image_count, grid_side // STRIPE, grid_side, STRIPE, model_width)
        values = jnp.transpose(image_grid, (0, 2, 1, 3, 4))
    return values.reshape(image_count, grid_side * grid_side, model_width)

def position_term(values, kernel, offset, grid_side, vertical):
    image_count, cell_count, model_width = values.shape
    image_grid = values.reshape(image_count, grid_side, grid_side, model_width)
    padded = jnp.pad(image_grid, ((0, 0), (1, 1), (1, 1), (0, 0)))
    stripe_place = jnp.arange(grid_side) % STRIPE
    upper_mask = (stripe_place != 0).astype(jnp.float32)
    lower_mask = (stripe_place != STRIPE - 1).astype(jnp.float32)
    accumulated = jnp.zeros_like(image_grid) + offset
    for row_step in range(3):
        for col_step in range(3):
            shifted = padded[:, row_step:row_step + grid_side, col_step:col_step + grid_side] * kernel[3 * row_step + col_step]
            stripe_step = col_step if vertical else row_step
            if stripe_step != 1:
                keep_mask = upper_mask if stripe_step == 0 else lower_mask
                mask_shape = (1, 1, grid_side, 1) if vertical else (1, grid_side, 1, 1)
                shifted = shifted * keep_mask.reshape(mask_shape)
            accumulated = accumulated + shifted
    return accumulated.reshape(image_count, cell_count, model_width)

def attend(query_rows, key_rows, value_rows):
    score_scale = query_rows.shape[-1] ** (-0.5)
    scores = low_back(jnp.einsum('bqhe,bkhe->bhqk', query_rows, key_rows, precision=lax.Precision.HIGHEST) * score_scale)
    row_max = lax.optimization_barrier(jnp.max(scores, axis=-1, keepdims=True))
    exponent = jnp.exp(scores - row_max)
    probabilities = low(exponent / lax.optimization_barrier(jnp.sum(exponent, axis=-1, keepdims=True)))
    return jnp.einsum('bhqk,bkhe->bqhe', probabilities, value_rows, precision=lax.Precision.HIGHEST)

def mixer(query_rows, key_rows, value_rows, kernel, offset, grid_side):
    image_count, cell_count, model_width = query_rows.shape
    half_width = model_width // 2
    head_count = HEADS // 2
    results = []
    for branch_index, vertical in enumerate((False, True)):
        channel_part = slice(branch_index * half_width, (branch_index + 1) * half_width)
        pieces = [to_stripes(tensor[..., channel_part], grid_side, vertical) for tensor in (query_rows, key_rows, value_rows)]
        pieces = [tensor.reshape(tensor.shape[0], tensor.shape[1], head_count, half_width // head_count) for tensor in pieces]
        mixed_heads = attend(pieces[0], pieces[1], pieces[2])
        mixed_heads = mixed_heads.reshape(mixed_heads.shape[0], mixed_heads.shape[1], half_width)
        results.append(from_stripes(mixed_heads, image_count, grid_side, vertical) + position_term(value_rows[..., channel_part], kernel[:, channel_part], offset[channel_part], grid_side, vertical))
    return jnp.concatenate(results, axis=-1)

def block(parameters, inputs, grid_side):
    qkv_w, proj_w, fc1_w, fc2_w, vectors = [low(tensor) for tensor in parameters]
    model_width = vectors.shape[1]
    normed = low(layer_norm(inputs, vectors[0], vectors[1]))
    joint_proj = matmul_high(normed, qkv_w)
    query_rows = low(low_back(joint_proj[..., :model_width] + vectors[2]))
    key_rows = low(low_back(joint_proj[..., model_width:2 * model_width]))
    value_rows = low(low_back(joint_proj[..., 2 * model_width:] + vectors[3]))
    mixed = low(low_back(mixer(query_rows, key_rows, value_rows, vectors[9:18], vectors[8], grid_side)))
    middle = inputs + low_back(matmul_high(mixed, proj_w) + vectors[4])
    normed_two = low(layer_norm(middle, vectors[5], vectors[6]))
    hidden = low_back(matmul_high(normed_two, fc1_w) + vectors[18:].reshape(-1))
    active = low(jax.nn.gelu(hidden, approximate=False))
    return middle + low_back(matmul_high(active, fc2_w) + vectors[7])

def adamw_update(weight, first, second, gradient, rate, decay):
    first = beta_one * first + (1.0 - beta_one) * gradient
    second = beta_two * second + (1.0 - beta_two) * gradient * gradient
    first_hat = first / (1.0 - beta_one ** STEP)
    second_hat = second / (1.0 - beta_two ** STEP)
    weight = weight - rate * (first_hat / (jnp.sqrt(second_hat) + adam_epsilon) + decay * weight)
    return (weight, first, second)

def reference(small_images, large_images, small_cot, large_cot, counts, qkv_master, qkv_first, qkv_second, proj_master, proj_first, proj_second, fc1_master, fc1_first, fc1_second, fc2_master, fc2_first, fc2_second, vec_master, vec_first, vec_second):
    parameters = (qkv_master, proj_master, fc1_master, fc2_master, vec_master)

    def run_bucket(images, cotangent, column, group_size):
        image_count, cell_count, model_width = images.shape
        grid_side = math.isqrt(cell_count)
        slot_count = image_count // counts.shape[0]
        live_mask = (jnp.arange(slot_count, dtype=jnp.int32)[None, :] < counts[:, column:column + 1]).reshape(-1).astype(jnp.float32)
        inputs = images.astype(jnp.float32).reshape(image_count // group_size, group_size, cell_count, model_width)
        cot_in = (cotangent.astype(jnp.float32) * live_mask[:, None, None]).reshape(image_count // group_size, group_size, cell_count, model_width)

        def scan_step(running, scan_item):
            values, cot_values = scan_item
            result, pullback = jax.vjp(lambda params_in, values_in: block(params_in, values_in, grid_side), parameters, values)
            param_grads, input_grads = pullback(cot_values)
            return (jax.tree.map(jnp.add, running, param_grads), (result, input_grads))
        zero_grads = jax.tree.map(jnp.zeros_like, parameters)
        running, (results, input_grads) = lax.scan(scan_step, zero_grads, (inputs, cot_in))
        results = results.reshape(image_count, cell_count, model_width) * live_mask[:, None, None]
        return (running, results, input_grads.reshape(image_count, cell_count, model_width))
    small_grads, small_result, small_back = run_bucket(small_images, small_cot, 0, 16)
    large_grads, large_result, large_back = run_bucket(large_images, large_cot, 1, 4)
    gradients = jax.tree.map(jnp.add, small_grads, large_grads)
    squares = jnp.float32(0.0)
    for gradient in gradients:
        squares = squares + jnp.sum(gradient * gradient)
    grad_total = jnp.sqrt(squares)
    clip_factor = jnp.minimum(1.0, clip_norm / (grad_total + 1e-06))
    qkv_new, qkv_first_new, qkv_second_new = adamw_update(qkv_master, qkv_first, qkv_second, gradients[0] * clip_factor, rate_matrix, decay_matrix)
    proj_new, proj_first_new, proj_second_new = adamw_update(proj_master, proj_first, proj_second, gradients[1] * clip_factor, rate_matrix, decay_matrix)
    fc1_new, fc1_first_new, fc1_second_new = adamw_update(fc1_master, fc1_first, fc1_second, gradients[2] * clip_factor, rate_matrix, decay_matrix)
    fc2_new, fc2_first_new, fc2_second_new = adamw_update(fc2_master, fc2_first, fc2_second, gradients[3] * clip_factor, rate_matrix, decay_matrix)
    vec_new, vec_first_new, vec_second_new = adamw_update(vec_master, vec_first, vec_second, gradients[4] * clip_factor, rate_vector, 0.0)
    return (small_result.astype(jnp.bfloat16), large_result.astype(jnp.bfloat16), small_back, large_back, qkv_new, qkv_first_new, qkv_second_new, qkv_new.astype(jnp.bfloat16), proj_new, proj_first_new, proj_second_new, proj_new.astype(jnp.bfloat16), fc1_new, fc1_first_new, fc1_second_new, fc1_new.astype(jnp.bfloat16), fc2_new, fc2_first_new, fc2_second_new, fc2_new.astype(jnp.bfloat16), vec_new, vec_first_new, vec_second_new, vec_new.astype(jnp.bfloat16), grad_total)
```

```python
import functools
import math

import jax
import jax.numpy as jnp
from jax import lax
from jax.experimental import pallas as pl
from jax.experimental.pallas import tpu as pltpu
from jax.sharding import PartitionSpec as P

HEADS = 8
STRIPE = 7
STEP = 10
LANES = 128

epsilon = 1e-05
clip_norm = 1.0
beta_one = 0.5
beta_two = 0.5
rate_matrix = 0.1
rate_vector = 0.5
decay_matrix = 0.05
adam_epsilon = 1e-08

BF = jnp.bfloat16
F32 = jnp.float32
FAR = -1e30

TAIL = 0.36
TAIL_POLY = (
    0.143705181,
    0.141884706,
    0.139098811,
    0.0282579301,
    0.178465629,
    -0.177935249,
    0.0465224759,
)


def dot_nn(a, b):
    return lax.dot_general(a, b, (((1,), (0,)), ((), ())), preferred_element_type=F32)


def dot_nt(a, b):
    return lax.dot_general(a, b, (((1,), (1,)), ((), ())), preferred_element_type=F32)


def dot_tn(a, b):
    return lax.dot_general(a, b, (((0,), (0,)), ((), ())), preferred_element_type=F32)


def fold_rows(v):
    return jnp.sum(v.reshape(v.shape[0] // 8, 8, v.shape[1]), axis=0)


def row_mean(v):
    return jnp.sum(v, axis=-1, keepdims=True) * (1.0 / v.shape[-1])


def gelu_parts(u):
    magnitude = jnp.abs(u)
    t = 1.0 / (1.0 + TAIL * magnitude)
    bell = jnp.exp(-0.5 * u * u)
    poly = jnp.full_like(t, TAIL_POLY[-1])
    for c in TAIL_POLY[-2::-1]:
        poly = poly * t + c
    low_side = poly * t * bell
    phi = jnp.where(u >= 0.0, 1.0 - low_side, low_side)
    return u * phi, phi + u * bell * (1.0 / math.sqrt(2.0 * math.pi))


def shift_down(v, n):
    return jnp.concatenate([jnp.zeros((n, v.shape[1]), v.dtype), v[:-n]], axis=0)


def shift_up(v, n):
    return jnp.concatenate([v[n:], jnp.zeros((n, v.shape[1]), v.dtype)], axis=0)


class Shape:
    def __init__(self, side):
        self.side = side
        self.wide = -(-side // 16) * 16
        self.stripes = side // STRIPE
        self.rows = STRIPE * self.wide
        self.queries = -(-self.rows // LANES) * LANES
        self.all = side * self.wide
        self.deep = -(-self.all // LANES) * LANES
        self.square = self.wide * self.wide

    def scratch(self, d, ff):
        s = self
        both = 2 * s.stripes
        return {
            "raw": ((s.side * s.side, d), F32),
            "x": ((s.all, d), F32),
            "gy": ((s.all, d), F32),
            "n1": ((s.all, d), F32),
            "r1": ((s.all, LANES), F32),
            "out": ((s.all, d), F32),
            "dx1": ((s.all, d), F32),
            "tq": ((3, s.square, LANES), F32),
            "o": ((s.all + s.square, LANES), F32),
            "dq": ((3, s.all + s.square, LANES), F32),
            "tb": ((3, s.all, LANES), BF),
            "q": ((both, s.queries, 2 * LANES), BF),
            "k": ((both, s.queries, 2 * LANES), BF),
            "v": ((both, s.queries, LANES), BF),
            "da": ((both, s.queries, LANES), BF),
            "p": ((both, HEADS // 2, s.queries, s.queries), BF),
            "ds": ((HEADS // 2, s.queries, s.queries), BF),
            "h1": ((s.deep, d), BF),
            "a": ((s.deep, d), BF),
            "h2": ((s.deep, d), BF),
            "gyb": ((s.deep, d), BF),
            "e1": ((s.deep, d), BF),
            "z": ((s.deep, ff), BF),
            "du": ((s.deep, ff), BF),
            "dqkv": ((s.deep, 3 * d), BF),
        }


def head_masks(width):
    lane = lax.broadcasted_iota(jnp.int32, (1, width), 1)
    e = LANES // (HEADS // 2)
    return [
        jnp.where((lane // e == h) | (lane == LANES), 1.0, 0.0).astype(BF)
        for h in range(HEADS // 2)
    ]


def pick_heads(parts):
    e = LANES // (HEADS // 2)
    lane = lax.broadcasted_iota(jnp.int32, parts[0].shape, 1)
    out = parts[-1]
    for h in range(len(parts) - 2, -1, -1):
        out = jnp.where(lane < (h + 1) * e, parts[h], out)
    return out


def place_mask(s, width):
    row = lax.broadcasted_iota(jnp.int32, (s.rows, width), 0)
    return lax.rem(row, s.wide) < s.side


def start_scratch(s, b):
    for name in ("x", "gy", "tq", "o", "dq", "tb", "q", "k", "v", "da", "p", "ds"):
        b[name][...] = jnp.zeros(b[name].shape, b[name].dtype)
    for name in ("h1", "a", "h2", "gyb", "e1", "z", "du", "dqkv"):
        if s.deep > s.all:
            tail = (s.deep - s.all, b[name].shape[1])
            b[name][s.all :, :] = jnp.zeros(tail, BF)
    lane = lax.broadcasted_iota(jnp.int32, (s.rows, LANES), 1)
    one = jnp.where(lane == 0, 1.0, 0.0)
    far = jnp.where((lane == 0) & ~place_mask(s, LANES), FAR, 0.0)
    for sb in range(2 * s.stripes):
        b["q"][sb, 0 : s.rows, LANES:] = one.astype(BF)
        b["k"][sb, 0 : s.rows, LANES:] = far.astype(BF)


def conv_rows(v, taps, s, flip):
    before = pltpu.roll(v, 1, 0)
    after = pltpu.roll(v, v.shape[0] - 1, 0)
    sides = (after, v, before) if flip else (before, v, after)
    mixed = []
    for a in range(3):
        mixed.append(sides[0] * taps[a][0] + sides[1] * taps[a][1] + sides[2] * taps[a][2])
    if flip:
        return mixed[1] + shift_down(mixed[2], s.wide) + shift_up(mixed[0], s.wide)
    return mixed[1] + shift_down(mixed[0], s.wide) + shift_up(mixed[2], s.wide)


def image_step(s, b, x_ref, cot_ref, y_ref, dx_ref, w_ref, g_ref, vec, kern, gv, gk, gb1):
    d = x_ref.shape[-1]
    ff = 4 * d
    heads = HEADS // 2
    e = LANES // heads
    scale = e**-0.5
    o_qkv, o_proj, o_fc1, o_fc2 = 0, 3 * d, 4 * d, 4 * d + ff
    mask = place_mask(s, LANES)

    def rows_of(t):
        return pl.ds(pl.multiple_of(t * s.rows, 16), s.rows)

    for src, dst in ((x_ref, "x"), (cot_ref, "gy")):
        b["raw"][...] = src[0].astype(F32)
        for r in range(s.side):
            b[dst][r * s.wide : r * s.wide + s.side, :] = b["raw"][
                r * s.side : (r + 1) * s.side, :
            ]

    def phase_a(t, carry):
        rows = rows_of(t)
        x = b["x"][rows, :]
        centered = x - row_mean(x)
        inverse = lax.rsqrt(row_mean(centered * centered) + epsilon)
        n1 = centered * inverse
        b["n1"][rows, :] = n1
        b["r1"][rows, :] = jnp.broadcast_to(inverse, (s.rows, LANES))
        h1 = (n1 * vec[0:1, :] + vec[1:2, :]).astype(BF)
        b["h1"][rows, :] = h1
        joint = dot_nn(h1, w_ref[:, o_qkv : o_qkv + 3 * d])
        q = joint[:, 0:d] + vec[2:3, :]
        k = joint[:, d : 2 * d]
        v = joint[:, 2 * d :] + vec[3:4, :]
        b["q"][t, 0 : s.rows, 0:LANES] = q[:, 0:LANES].astype(BF)
        b["k"][t, 0 : s.rows, 0:LANES] = k[:, 0:LANES].astype(BF)
        b["v"][t, 0 : s.rows, :] = jnp.where(mask, v[:, 0:LANES], 0.0).astype(BF)
        b["tq"][0, rows, :] = q[:, LANES:]
        b["tq"][1, rows, :] = k[:, LANES:]
        b["tq"][2, rows, :] = v[:, LANES:]
        return carry

    lax.fori_loop(0, s.stripes, phase_a, 0)

    for which, name in enumerate(("q", "k", "v")):
        for c in range(s.side):
            piece = b["tq"][which, pl.ds(c, s.wide, stride=s.wide), :]
            b[name][
                s.stripes + c // STRIPE,
                s.wide * (c % STRIPE) : s.wide * (c % STRIPE + 1),
                0:LANES,
            ] = piece.astype(BF)

    def taps_of(branch):
        rows9 = kern[branch]
        return [[rows9[3 * a + c : 3 * a + c + 1, :] for c in range(3)] for a in range(3)], rows9[
            9:10, :
        ]

    masks_wide = head_masks(2 * LANES)
    masks_one = head_masks(LANES)

    def phase_b(sb, carry):
        q = b["q"][sb]
        k = b["k"][sb, 0 : s.rows, :]
        k4 = jnp.concatenate([k * m for m in masks_wide], axis=0)
        s4 = dot_nt(k4, q)
        v = b["v"][sb].astype(F32)
        vt = jnp.transpose(v).astype(BF)
        parts = []
        for h in range(heads):
            sh = s4[h * s.rows : (h + 1) * s.rows, :]
            top = jnp.max(sh, axis=0, keepdims=True)
            ex = jnp.exp((sh - top) * scale)
            total = jnp.sum(ex, axis=0, keepdims=True)
            b["p"][sb, h, 0 : s.rows, :] = (ex * (1.0 / total)).astype(BF)
            parts.append(dot_nn(vt[h * e : (h + 1) * e, :], b["p"][sb, h]))
        o = jnp.transpose(jnp.concatenate(parts, axis=0))[0 : s.rows, :]
        taps, offset = taps_of(sb // s.stripes)
        pos = conv_rows(v[0 : s.rows, :], taps, s, False) + offset
        b["o"][rows_of(sb), :] = o + pos
        return carry

    lax.fori_loop(0, 2 * s.stripes, phase_b, 0)

    def turn_back(src_at, dst_at):
        for r in range(s.side):
            piece = src_at(pl.ds(s.all + r, s.wide, stride=s.wide))
            dst_at(slice(s.wide * r, s.wide * (r + 1)), piece.astype(BF))

    def put_a(rows, piece):
        b["a"][rows, LANES:] = piece

    turn_back(lambda rows: b["o"][rows, :], put_a)

    def phase_c(t, carry):
        rows = rows_of(t)
        b["a"][rows, 0:LANES] = b["o"][rows, :].astype(BF)
        x1 = b["x"][rows, :] + dot_nt(b["a"][rows, :], w_ref[:, o_proj : o_proj + d]) + vec[4:5, :]
        centered = x1 - row_mean(x1)
        inverse = lax.rsqrt(row_mean(centered * centered) + epsilon)
        n2 = centered * inverse
        h2 = (n2 * vec[5:6, :] + vec[6:7, :]).astype(BF)
        b["h2"][rows, :] = h2
        gy = b["gy"][rows, :]
        gyb = gy.astype(BF)
        b["gyb"][rows, :] = gyb
        out = x1 + vec[7:8, :]
        dh2 = jnp.zeros((s.rows, d), F32)
        for j in range(4):
            c1 = slice(o_fc1 + j * d, o_fc1 + (j + 1) * d)
            c2 = slice(o_fc2 + j * d, o_fc2 + (j + 1) * d)
            cj = slice(j * d, (j + 1) * d)
            u = dot_nn(h2, w_ref[:, c1]) + vec[18 + j : 19 + j, :]
            z, slope = gelu_parts(u)
            z = z.astype(BF)
            b["z"][rows, cj] = z
            out = out + dot_nt(z, w_ref[:, c2])
            du = (dot_nn(gyb, w_ref[:, c2]) * slope).astype(BF)
            b["du"][rows, cj] = du
            dh2 = dh2 + dot_nt(du, w_ref[:, c1])
            gb1[j] += fold_rows(du.astype(F32))
        b["out"][rows, :] = out
        dn = dh2 * vec[5:6, :]
        dx1 = gy + inverse * (dn - row_mean(dn) - n2 * row_mean(dn * n2))
        b["dx1"][rows, :] = dx1
        e1 = dx1.astype(BF)
        b["e1"][rows, :] = e1
        gv[5] += fold_rows(dh2 * n2)
        gv[6] += fold_rows(dh2)
        gv[7] += fold_rows(gy)
        gv[4] += fold_rows(e1.astype(F32))
        da = dot_nn(e1, w_ref[:, o_proj : o_proj + d])
        b["da"][t, 0 : s.rows, :] = da[:, 0:LANES].astype(BF)
        b["tq"][0, rows, :] = da[:, LANES:]
        return carry

    lax.fori_loop(0, s.stripes, phase_c, 0)

    for r in range(s.side):
        b["raw"][r * s.side : (r + 1) * s.side, :] = b["out"][
            r * s.wide : r * s.wide + s.side, :
        ]
    y_ref[0] = b["raw"][...].astype(BF)

    for c in range(s.side):
        piece = b["tq"][0, pl.ds(c, s.wide, stride=s.wide), :]
        b["da"][
            s.stripes + c // STRIPE, s.wide * (c % STRIPE) : s.wide * (c % STRIPE + 1), :
        ] = piece.astype(BF)

    def phase_d(sb, carry):
        branch = sb // s.stripes
        v = b["v"][sb, 0 : s.rows, :]
        da = b["da"][sb]
        v4 = jnp.concatenate([v * m for m in masks_one], axis=0)
        dp4 = dot_nt(v4, da)
        kt = jnp.transpose(b["k"][sb, :, 0:LANES].astype(F32)).astype(BF)
        parts = []
        for h in range(heads):
            ph = b["p"][sb, h, 0 : s.rows, :].astype(F32)
            pd = ph * dp4[h * s.rows : (h + 1) * s.rows, :]
            inner = jnp.sum(pd, axis=0, keepdims=True)
            b["ds"][h, 0 : s.rows, :] = (pd - ph * inner).astype(BF)
            parts.append(dot_nn(kt[h * e : (h + 1) * e, :], b["ds"][h]))
        dq = jnp.transpose(jnp.concatenate(parts, axis=0))[0 : s.rows, :] * scale
        ds4 = jnp.concatenate([b["ds"][h, 0 : s.rows, :] for h in range(heads)], axis=0)
        dk4 = dot_nn(ds4, b["q"][sb, :, 0:LANES])
        dk = pick_heads([dk4[h * s.rows : (h + 1) * s.rows, :] for h in range(heads)]) * scale
        p4 = jnp.concatenate([b["p"][sb, h, 0 : s.rows, :] for h in range(heads)], axis=0)
        dv4 = dot_nn(p4, da)
        dv = pick_heads([dv4[h * s.rows : (h + 1) * s.rows, :] for h in range(heads)])
        taps, offset = taps_of(branch)
        dac = da[0 : s.rows, :].astype(F32)
        vf = v.astype(F32)
        dv = jnp.where(mask, dv + conv_rows(dac, taps, s, True), 0.0)
        rows = rows_of(sb)
        b["dq"][0, rows, :] = dq
        b["dq"][1, rows, :] = dk
        b["dq"][2, rows, :] = dv
        sides = (pltpu.roll(vf, 1, 0), vf, pltpu.roll(vf, s.rows - 1, 0))
        for c in range(3):
            gk[branch, c] += fold_rows(dac[s.wide :] * sides[c][: -s.wide])
            gk[branch, 3 + c] += fold_rows(dac * sides[c])
            gk[branch, 6 + c] += fold_rows(dac[: -s.wide] * sides[c][s.wide :])
        gk[branch, 9] += fold_rows(dac)
        return carry

    lax.fori_loop(0, 2 * s.stripes, phase_d, 0)

    for which in range(3):

        def put_b(rows, piece, which=which):
            b["dqkv"][rows, which * d + LANES : (which + 1) * d] = piece

        turn_back(lambda rows, which=which: b["dq"][which, rows, :], put_b)

    def phase_e(t, carry):
        rows = rows_of(t)
        for which in range(3):
            b["dqkv"][rows, which * d : which * d + LANES] = b["dq"][which, rows, :].astype(BF)
        dqkv = b["dqkv"][rows, :]
        gv[2] += fold_rows(dqkv[:, 0:d].astype(F32))
        gv[3] += fold_rows(dqkv[:, 2 * d :].astype(F32))
        dh1 = dot_nt(dqkv, w_ref[:, o_qkv : o_qkv + 3 * d])
        n1 = b["n1"][rows, :]
        r1 = b["r1"][rows, :]
        dn = dh1 * vec[0:1, :]
        back = dn - row_mean(dn) - n1 * row_mean(dn * n1)
        b["out"][rows, :] = b["dx1"][rows, :] + back * jnp.concatenate([r1, r1], axis=1)
        gv[0] += fold_rows(dh1 * n1)
        gv[1] += fold_rows(dh1)
        return carry

    lax.fori_loop(0, s.stripes, phase_e, 0)

    for r in range(s.side):
        dx_ref[0, r * s.side : (r + 1) * s.side, :] = b["out"][
            r * s.wide : r * s.wide + s.side, :
        ]

    for left, right, start, width in (
        ("h1", "dqkv", o_qkv, 3 * d),
        ("e1", "a", o_proj, d),
        ("h2", "du", o_fc1, ff),
        ("gyb", "z", o_fc2, ff),
    ):
        turned = b[left][...]
        for j in range(0, width, d):
            g_ref[:, start + j : start + j + d] += dot_tn(turned, b[right][:, j : j + d])


def block_kernel(names, sizes, small, large, counts, xs, xl, cs, cl, w_ref, *rest):
    ys, yl, ds, dl, g_ref = rest[:5]
    vec, kern, gv, gk, gb1 = rest[5:10]
    scratch = rest[10:]
    few = dict(zip(names[: sizes[0]], scratch[: sizes[0]]))
    many = dict(zip(names[sizes[0] :], scratch[sizes[0] :]))
    step = pl.program_id(0)
    d = xs.shape[-1]
    small_steps = sizes[1]
    small_shape, large_shape = small, large

    @pl.when(step == 0)
    def _():
        start_scratch(small_shape, few)
        start_scratch(large_shape, many)
        for ref in (gv, gk, gb1, g_ref):
            ref[...] = jnp.zeros(ref.shape, ref.dtype)
        vec[...] = jnp.transpose(w_ref[:, 12 * d :].astype(F32))[0:32, :]
        for branch in range(2):
            lanes = slice(branch * LANES, (branch + 1) * LANES)
            for a in range(3):
                for c in range(3):
                    row = 9 + (3 * c + a if branch else 3 * a + c)
                    kern[branch, 3 * a + c : 3 * a + c + 1, :] = vec[row : row + 1, lanes]
            kern[branch, 9:10, :] = vec[8:9, lanes]

    def one(s, b, slot, live, x_ref, cot_ref, y_ref, dx_ref):
        @pl.when(slot < live)
        def _():
            image_step(s, b, x_ref, cot_ref, y_ref, dx_ref, w_ref, g_ref, vec, kern, gv, gk, gb1)

        @pl.when(slot >= live)
        def _():
            y_ref[...] = jnp.zeros(y_ref.shape, y_ref.dtype)
            dx_ref[...] = jnp.zeros(dx_ref.shape, dx_ref.dtype)

    @pl.when(step < small_steps)
    def _():
        one(small_shape, few, step, counts[0, 0], xs, cs, ys, ds)

    @pl.when(step >= small_steps)
    def _():
        one(large_shape, many, step - small_steps, counts[0, 1], xl, cl, yl, dl)

    @pl.when(step == pl.num_programs(0) - 1)
    def _():
        rows = []
        for i in range(8):
            rows.append(jnp.sum(gv[i], axis=0, keepdims=True))

        def taps_row(index, branch):
            return jnp.sum(gk[branch, index], axis=0, keepdims=True)

        rows.append(jnp.concatenate([taps_row(9, 0), taps_row(9, 1)], axis=1))
        for a in range(3):
            for c in range(3):
                rows.append(
                    jnp.concatenate([taps_row(3 * a + c, 0), taps_row(3 * c + a, 1)], axis=1)
                )
        for j in range(4):
            rows.append(jnp.sum(gb1[j], axis=0, keepdims=True))
        rows.append(jnp.zeros((LANES - len(rows), d), F32))
        g_ref[:, 12 * d :] = jnp.transpose(jnp.concatenate(rows, axis=0))


def run_block(small_images, large_images, small_cot, large_cot, counts, weights):
    few, small_cells, d = small_images.shape
    many, large_cells, _ = large_images.shape
    small = Shape(math.isqrt(small_cells))
    large = Shape(math.isqrt(large_cells))
    width = weights.shape[1]
    small_scratch = small.scratch(d, 4 * d)
    large_scratch = large.scratch(d, 4 * d)
    names = tuple(small_scratch) + tuple(large_scratch)
    spaces = [
        pltpu.VMEM(shape, dtype)
        for shape, dtype in list(small_scratch.values()) + list(large_scratch.values())
    ]

    def small_at(i):
        return (jnp.minimum(i, few - 1), 0, 0)

    def large_at(i):
        return (jnp.maximum(i - few, 0), 0, 0)

    small_block = pl.BlockSpec((1, small_cells, d), small_at)
    large_block = pl.BlockSpec((1, large_cells, d), large_at)
    whole = pl.BlockSpec((d, width), lambda i: (0, 0), pipeline_mode=pl.Buffered(1))
    return pl.pallas_call(
        functools.partial(block_kernel, names, (len(small_scratch), few), small, large),
        grid=(few + many,),
        in_specs=[
            pl.BlockSpec(memory_space=pltpu.SMEM),
            small_block,
            large_block,
            small_block,
            large_block,
            whole,
        ],
        out_specs=[small_block, large_block, small_block, large_block, whole],
        out_shape=[
            jax.ShapeDtypeStruct(small_images.shape, BF),
            jax.ShapeDtypeStruct(large_images.shape, BF),
            jax.ShapeDtypeStruct(small_images.shape, F32),
            jax.ShapeDtypeStruct(large_images.shape, F32),
            jax.ShapeDtypeStruct((d, width), F32),
        ],
        scratch_shapes=[
            pltpu.VMEM((32, d), F32),
            pltpu.VMEM((2, 16, LANES), F32),
            pltpu.VMEM((8, 8, d), F32),
            pltpu.VMEM((2, 16, 8, LANES), F32),
            pltpu.VMEM((4, 8, d), F32),
        ]
        + spaces,
        compiler_params=pltpu.CompilerParams(
            dimension_semantics=("arbitrary",), vmem_limit_bytes=60 * 2**20
        ),
    )(counts, small_images, large_images, small_cot, large_cot, weights)


def adamw_update(weight, first, second, gradient, rate, decay):
    first = beta_one * first + (1.0 - beta_one) * gradient
    second = beta_two * second + (1.0 - beta_two) * gradient * gradient
    first_hat = first / (1.0 - beta_one**STEP)
    second_hat = second / (1.0 - beta_two**STEP)
    weight = weight - rate * (first_hat / (jnp.sqrt(second_hat) + adam_epsilon) + decay * weight)
    return (weight, first, second)


AXES = ("dp", "fsdp")


def on_device(
    small_images,
    large_images,
    small_cot,
    large_cot,
    counts,
    *state,
):
    masters = [state[i] for i in range(0, 15, 3)]
    turned = (False, True, False, True, True)
    d = small_images.shape[-1]
    own = [m.T if t else m for m, t in zip(masters, turned)]
    shard_rows = own[0].shape[0]
    pad = jnp.zeros((shard_rows, LANES - own[4].shape[1]), F32)
    packed = jnp.concatenate(own + [pad], axis=1).astype(BF)
    weights = lax.all_gather(packed, AXES, axis=0, tiled=True)
    small_out, large_out, small_back, large_back, grads = run_block(
        small_images, large_images, small_cot, large_cot, counts, weights
    )
    shard = lax.psum_scatter(grads, AXES, scatter_dimension=0, tiled=True)
    total = jnp.sqrt(lax.psum(jnp.sum(shard * shard), AXES))
    clip_factor = jnp.minimum(1.0, clip_norm / (total + 1e-06))
    outs = [small_out, large_out, small_back, large_back]
    place = 0
    for i, t in enumerate(turned):
        master, first, second = state[3 * i : 3 * i + 3]
        width = own[i].shape[1]
        part = shard[:, place : place + width]
        place += width
        grad = (part.T if t else part) * clip_factor
        rate, decay = (rate_vector, 0.0) if i == 4 else (rate_matrix, decay_matrix)
        new, first_new, second_new = adamw_update(master, first, second, grad, rate, decay)
        outs += [new, first_new, second_new, new.astype(BF)]
    return (*outs, total)


def solution(mesh):
    cells = P(AXES, None, None)
    rows = P(AXES, None)
    columns = P(None, AXES)
    weights = [rows, columns, rows, columns, columns]
    return jax.shard_map(
        on_device,
        mesh=mesh,
        in_specs=(cells,) * 4 + (rows,) + tuple(w for w in weights for _ in range(3)),
        out_specs=(cells,) * 4 + tuple(w for w in weights for _ in range(4)) + (P(),),
        check_vma=False,
    )
```

```python
import functools
import math

import jax
import jax.numpy as jnp
from jax import lax
from jax.experimental import pallas as pl
from jax.experimental.pallas import tpu as pltpu
from jax.sharding import PartitionSpec as P

HEADS = 8
STRIPE = 7
STEP = 10
LANES = 128

epsilon = 1e-05
clip_norm = 1.0
beta_one = 0.5
beta_two = 0.5
rate_matrix = 0.1
rate_vector = 0.5
decay_matrix = 0.05
adam_epsilon = 1e-08

BF = jnp.bfloat16
F32 = jnp.float32
FAR = -1e30
SKIP = set()


def dot_nn(a, b):
    return lax.dot_general(a, b, (((1,), (0,)), ((), ())), preferred_element_type=F32)


def dot_nt(a, b):
    return lax.dot_general(a, b, (((1,), (1,)), ((), ())), preferred_element_type=F32)


def dot_tn(a, b):
    return lax.dot_general(a, b, (((0,), (0,)), ((), ())), preferred_element_type=F32)


def fold_rows(v):
    return jnp.sum(v.reshape(v.shape[0] // 8, 8, v.shape[1]), axis=0)


def row_mean(v):
    return jnp.sum(v, axis=-1, keepdims=True) * (1.0 / v.shape[-1])


def gelu_parts(u):
    phi = 0.5 * lax.erf(u * math.sqrt(0.5)) + 0.5
    bell = jnp.exp(-0.5 * u * u)
    return u * phi, phi + u * bell * (1.0 / math.sqrt(2.0 * math.pi))


def shift_down(v, n):
    return jnp.concatenate([jnp.zeros((n, v.shape[1]), v.dtype), v[:-n]], axis=0)


def shift_up(v, n):
    return jnp.concatenate([v[n:], jnp.zeros((n, v.shape[1]), v.dtype)], axis=0)


class Shape:
    def __init__(self, side):
        self.side = side
        self.wide = -(-side // 16) * 16
        self.stripes = side // STRIPE
        self.rows = STRIPE * self.wide
        self.queries = -(-self.rows // LANES) * LANES
        self.all = side * self.wide
        self.deep = -(-self.all // LANES) * LANES
        self.square = self.wide * self.wide

    def scratch(self, d, ff):
        s = self
        both = 2 * s.stripes
        return {
            "raw": ((s.side * s.side, d), F32),
            "x": ((s.all, d), F32),
            "gy": ((s.all, d), F32),
            "n1": ((s.all, d), F32),
            "r1": ((s.all, LANES), F32),
            "out": ((s.all, d), F32),
            "dx1": ((s.all, d), F32),
            "tq": ((3, s.square, LANES), F32),
            "o": ((s.all + s.square, LANES), F32),
            "dq": ((3, s.all + s.square, LANES), F32),
            "q": ((both, s.queries, 2 * LANES), BF),
            "k": ((both, s.queries, 2 * LANES), BF),
            "v": ((both, s.queries, LANES), BF),
            "da": ((both, s.queries, LANES), BF),
            "p": ((both, HEADS // 2, s.queries, s.queries), BF),
            "ds": ((HEADS // 2, s.queries, s.queries), BF),
            "h1": ((s.deep, d), BF),
            "a": ((s.deep, d), BF),
            "h2": ((s.deep, d), BF),
            "gyb": ((s.deep, d), BF),
            "e1": ((s.deep, d), BF),
            "z": ((s.deep, ff), BF),
            "du": ((s.deep, ff), BF),
            "dqkv": ((s.deep, 3 * d), BF),
        }


def head_masks(width):
    lane = lax.broadcasted_iota(jnp.int32, (1, width), 1)
    e = LANES // (HEADS // 2)
    return [
        jnp.where((lane // e == h) | (lane == LANES), 1.0, 0.0).astype(BF)
        for h in range(HEADS // 2)
    ]


def pick_heads(parts):
    e = LANES // (HEADS // 2)
    lane = lax.broadcasted_iota(jnp.int32, parts[0].shape, 1)
    out = parts[-1]
    for h in range(len(parts) - 2, -1, -1):
        out = jnp.where(lane < (h + 1) * e, parts[h], out)
    return out


def place_mask(s, width):
    row = lax.broadcasted_iota(jnp.int32, (s.rows, width), 0)
    return lax.rem(row, s.wide) < s.side


def start_scratch(s, b):
    for name in ("x", "gy"):
        b[name][...] = jnp.zeros(b[name].shape, F32)
    tail = jnp.zeros((s.square - s.all, LANES), F32)
    for which in range(3):
        b["tq"][which, s.all :, :] = tail
        b["dq"][which, 2 * s.all :, :] = tail
    b["o"][2 * s.all :, :] = tail
    extra = s.queries - s.rows
    for sb in range(2 * s.stripes):
        for name in ("q", "k", "v", "da"):
            b[name][sb, s.rows :, :] = jnp.zeros((extra, b[name].shape[2]), BF)
        for h in range(HEADS // 2):
            b["p"][sb, h, s.rows :, :] = jnp.zeros((extra, s.queries), BF)
    for h in range(HEADS // 2):
        b["ds"][h, s.rows :, :] = jnp.zeros((extra, s.queries), BF)
    for name in ("h1", "a", "h2", "gyb", "e1", "z", "du", "dqkv"):
        if s.deep > s.all:
            tail = (s.deep - s.all, b[name].shape[1])
            b[name][s.all :, :] = jnp.zeros(tail, BF)
    lane = lax.broadcasted_iota(jnp.int32, (s.rows, LANES), 1)
    one = jnp.where(lane == 0, 1.0, 0.0)
    far = jnp.where((lane == 0) & ~place_mask(s, LANES), FAR, 0.0)
    for sb in range(2 * s.stripes):
        b["q"][sb, 0 : s.rows, LANES:] = one.astype(BF)
        b["k"][sb, 0 : s.rows, LANES:] = far.astype(BF)


def conv_rows(v, taps, s, flip):
    before = pltpu.roll(v, 1, 0)
    after = pltpu.roll(v, v.shape[0] - 1, 0)
    sides = (after, v, before) if flip else (before, v, after)
    mixed = []
    for a in range(3):
        mixed.append(sides[0] * taps[a][0] + sides[1] * taps[a][1] + sides[2] * taps[a][2])
    if flip:
        return mixed[1] + shift_down(mixed[2], s.wide) + shift_up(mixed[0], s.wide)
    return mixed[1] + shift_down(mixed[0], s.wide) + shift_up(mixed[2], s.wide)


def image_step(s, b, x_ref, cot_ref, y_ref, dx_ref, w_ref, g_ref, vec, kern, gv, gk, gb1):
    d = x_ref.shape[-1]
    ff = 4 * d
    heads = HEADS // 2
    e = LANES // heads
    scale = e**-0.5
    o_qkv, o_proj, o_fc1, o_fc2 = 0, 3 * d, 4 * d, 4 * d + ff
    mask = place_mask(s, LANES)

    def rows_of(t):
        return pl.ds(pl.multiple_of(t * s.rows, 16), s.rows)

    for src, dst in ((x_ref, "x"), (cot_ref, "gy")):
        b["raw"][...] = src[0].astype(F32)
        for r in range(s.side):
            b[dst][r * s.wide : r * s.wide + s.side, :] = b["raw"][
                r * s.side : (r + 1) * s.side, :
            ]

    def phase_a(t, carry):
        rows = rows_of(t)
        x = b["x"][rows, :]
        centered = x - row_mean(x)
        inverse = lax.rsqrt(row_mean(centered * centered) + epsilon)
        n1 = centered * inverse
        b["n1"][rows, :] = n1
        b["r1"][rows, :] = jnp.broadcast_to(inverse, (s.rows, LANES))
        h1 = (n1 * vec[0:1, :] + vec[1:2, :]).astype(BF)
        b["h1"][rows, :] = h1
        joint = dot_nn(h1, w_ref[:, o_qkv : o_qkv + 3 * d])
        q = joint[:, 0:d] + vec[2:3, :]
        k = joint[:, d : 2 * d]
        v = joint[:, 2 * d :] + vec[3:4, :]
        b["q"][t, 0 : s.rows, 0:LANES] = q[:, 0:LANES].astype(BF)
        b["k"][t, 0 : s.rows, 0:LANES] = k[:, 0:LANES].astype(BF)
        b["v"][t, 0 : s.rows, :] = jnp.where(mask, v[:, 0:LANES], 0.0).astype(BF)
        b["tq"][0, rows, :] = q[:, LANES:]
        b["tq"][1, rows, :] = k[:, LANES:]
        b["tq"][2, rows, :] = v[:, LANES:]
        return carry

    lax.fori_loop(0, 0 if 'a' in SKIP else s.stripes, phase_a, 0, unroll=True)

    for which, name in enumerate(("q", "k", "v")):
        for c in range(0 if 't' in SKIP else s.side):
            piece = b["tq"][which, pl.ds(c, s.wide, stride=s.wide), :]
            b[name][
                s.stripes + c // STRIPE,
                s.wide * (c % STRIPE) : s.wide * (c % STRIPE + 1),
                0:LANES,
            ] = piece.astype(BF)

    def taps_of(branch):
        rows9 = kern[branch]
        return [[rows9[3 * a + c : 3 * a + c + 1, :] for c in range(3)] for a in range(3)], rows9[
            9:10, :
        ]

    masks_wide = head_masks(2 * LANES)
    masks_one = head_masks(LANES)

    def phase_b(sb, carry):
        q = b["q"][sb]
        k = b["k"][sb, 0 : s.rows, :]
        k4 = jnp.concatenate([k * m for m in masks_wide], axis=0)
        s4 = dot_nt(k4, q)
        v = b["v"][sb].astype(F32)
        vt = jnp.transpose(v).astype(BF)
        parts = []
        for h in range(heads):
            sh = s4[h * s.rows : (h + 1) * s.rows, :]
            top = jnp.max(sh, axis=0, keepdims=True)
            ex = jnp.exp((sh - top) * scale)
            total = jnp.sum(ex, axis=0, keepdims=True)
            b["p"][sb, h, 0 : s.rows, :] = (ex * (1.0 / total)).astype(BF)
            parts.append(dot_nn(vt[h * e : (h + 1) * e, :], b["p"][sb, h]))
        o = jnp.transpose(jnp.concatenate(parts, axis=0))[0 : s.rows, :]
        taps, offset = taps_of(sb // s.stripes)
        pos = conv_rows(v[0 : s.rows, :], taps, s, False) + offset
        b["o"][rows_of(sb), :] = o + pos
        return carry

    lax.fori_loop(0, 0 if 'b' in SKIP else 2 * s.stripes, phase_b, 0, unroll=True)

    def turn_back(src_at, dst_at):
        for r in range(0 if 't' in SKIP else s.side):
            piece = src_at(pl.ds(s.all + r, s.wide, stride=s.wide))
            dst_at(slice(s.wide * r, s.wide * (r + 1)), piece.astype(BF))

    def put_a(rows, piece):
        b["a"][rows, LANES:] = piece

    turn_back(lambda rows: b["o"][rows, :], put_a)

    def phase_c(t, carry):
        rows = rows_of(t)
        b["a"][rows, 0:LANES] = b["o"][rows, :].astype(BF)
        x1 = b["x"][rows, :] + dot_nt(b["a"][rows, :], w_ref[:, o_proj : o_proj + d]) + vec[4:5, :]
        centered = x1 - row_mean(x1)
        inverse = lax.rsqrt(row_mean(centered * centered) + epsilon)
        n2 = centered * inverse
        h2 = (n2 * vec[5:6, :] + vec[6:7, :]).astype(BF)
        b["h2"][rows, :] = h2
        gy = b["gy"][rows, :]
        gyb = gy.astype(BF)
        b["gyb"][rows, :] = gyb
        out = x1 + vec[7:8, :]
        dh2 = jnp.zeros((s.rows, d), F32)
        for j in range(4):
            c1 = slice(o_fc1 + j * d, o_fc1 + (j + 1) * d)
            c2 = slice(o_fc2 + j * d, o_fc2 + (j + 1) * d)
            cj = slice(j * d, (j + 1) * d)
            u = dot_nn(h2, w_ref[:, c1]) + vec[18 + j : 19 + j, :]
            z, slope = gelu_parts(u)
            z = z.astype(BF)
            b["z"][rows, cj] = z
            out = out + dot_nt(z, w_ref[:, c2])
            du = (dot_nn(gyb, w_ref[:, c2]) * slope).astype(BF)
            b["du"][rows, cj] = du
            dh2 = dh2 + dot_nt(du, w_ref[:, c1])
            gb1[j] += fold_rows(du.astype(F32))
        b["out"][rows, :] = out
        dn = dh2 * vec[5:6, :]
        dx1 = gy + inverse * (dn - row_mean(dn) - n2 * row_mean(dn * n2))
        b["dx1"][rows, :] = dx1
        e1 = dx1.astype(BF)
        b["e1"][rows, :] = e1
        gv[5] += fold_rows(dh2 * n2)
        gv[6] += fold_rows(dh2)
        gv[7] += fold_rows(gy)
        gv[4] += fold_rows(e1.astype(F32))
        da = dot_nn(e1, w_ref[:, o_proj : o_proj + d])
        b["da"][t, 0 : s.rows, :] = da[:, 0:LANES].astype(BF)
        b["tq"][0, rows, :] = da[:, LANES:]
        return carry

    lax.fori_loop(0, 0 if 'c' in SKIP else s.stripes, phase_c, 0, unroll=True)

    for r in range(s.side):
        b["raw"][r * s.side : (r + 1) * s.side, :] = b["out"][
            r * s.wide : r * s.wide + s.side, :
        ]
    y_ref[0] = b["raw"][...].astype(BF)

    for c in range(s.side):
        piece = b["tq"][0, pl.ds(c, s.wide, stride=s.wide), :]
        b["da"][
            s.stripes + c // STRIPE, s.wide * (c % STRIPE) : s.wide * (c % STRIPE + 1), :
        ] = piece.astype(BF)

    def phase_d(sb, carry):
        branch = sb // s.stripes
        v = b["v"][sb, 0 : s.rows, :]
        da = b["da"][sb]
        v4 = jnp.concatenate([v * m for m in masks_one], axis=0)
        dp4 = dot_nt(v4, da)
        kt = jnp.transpose(b["k"][sb, :, 0:LANES].astype(F32)).astype(BF)
        parts = []
        for h in range(heads):
            ph = b["p"][sb, h, 0 : s.rows, :].astype(F32)
            pd = ph * dp4[h * s.rows : (h + 1) * s.rows, :]
            inner = jnp.sum(pd, axis=0, keepdims=True)
            b["ds"][h, 0 : s.rows, :] = (pd - ph * inner).astype(BF)
            parts.append(dot_nn(kt[h * e : (h + 1) * e, :], b["ds"][h]))
        dq = jnp.transpose(jnp.concatenate(parts, axis=0))[0 : s.rows, :] * scale
        ds4 = jnp.concatenate([b["ds"][h, 0 : s.rows, :] for h in range(heads)], axis=0)
        dk4 = dot_nn(ds4, b["q"][sb, :, 0:LANES])
        dk = pick_heads([dk4[h * s.rows : (h + 1) * s.rows, :] for h in range(heads)]) * scale
        p4 = jnp.concatenate([b["p"][sb, h, 0 : s.rows, :] for h in range(heads)], axis=0)
        dv4 = dot_nn(p4, da)
        dv = pick_heads([dv4[h * s.rows : (h + 1) * s.rows, :] for h in range(heads)])
        taps, offset = taps_of(branch)
        dac = da[0 : s.rows, :].astype(F32)
        vf = v.astype(F32)
        dv = jnp.where(mask, dv + conv_rows(dac, taps, s, True), 0.0)
        rows = rows_of(sb)
        b["dq"][0, rows, :] = dq
        b["dq"][1, rows, :] = dk
        b["dq"][2, rows, :] = dv
        sides = (pltpu.roll(vf, 1, 0), vf, pltpu.roll(vf, s.rows - 1, 0))
        for c in range(3):
            gk[branch, c] += fold_rows(dac[s.wide :] * sides[c][: -s.wide])
            gk[branch, 3 + c] += fold_rows(dac * sides[c])
            gk[branch, 6 + c] += fold_rows(dac[: -s.wide] * sides[c][s.wide :])
        gk[branch, 9] += fold_rows(dac)
        return carry

    lax.fori_loop(0, 0 if 'd' in SKIP else 2 * s.stripes, phase_d, 0, unroll=True)

    for which in range(3):

        def put_b(rows, piece, which=which):
            b["dqkv"][rows, which * d + LANES : (which + 1) * d] = piece

        turn_back(lambda rows, which=which: b["dq"][which, rows, :], put_b)

    def phase_e(t, carry):
        rows = rows_of(t)
        for which in range(3):
            b["dqkv"][rows, which * d : which * d + LANES] = b["dq"][which, rows, :].astype(BF)
        dqkv = b["dqkv"][rows, :]
        gv[2] += fold_rows(dqkv[:, 0:d].astype(F32))
        gv[3] += fold_rows(dqkv[:, 2 * d :].astype(F32))
        dh1 = dot_nt(dqkv, w_ref[:, o_qkv : o_qkv + 3 * d])
        n1 = b["n1"][rows, :]
        r1 = b["r1"][rows, :]
        dn = dh1 * vec[0:1, :]
        back = dn - row_mean(dn) - n1 * row_mean(dn * n1)
        b["out"][rows, :] = b["dx1"][rows, :] + back * jnp.concatenate([r1, r1], axis=1)
        gv[0] += fold_rows(dh1 * n1)
        gv[1] += fold_rows(dh1)
        return carry

    lax.fori_loop(0, 0 if 'e' in SKIP else s.stripes, phase_e, 0, unroll=True)

    for r in range(s.side):
        dx_ref[0, r * s.side : (r + 1) * s.side, :] = b["out"][
            r * s.wide : r * s.wide + s.side, :
        ]

    for left, right, start, width in (
        ("h1", "dqkv", o_qkv, 3 * d),
        ("e1", "a", o_proj, d),
        ("h2", "du", o_fc1, ff),
        ("gyb", "z", o_fc2, ff),
    ):
        if 'f' in SKIP: break
        turned = b[left][...]
        for j in range(0, width, d):
            g_ref[:, start + j : start + j + d] += dot_tn(turned, b[right][:, j : j + d])


def place_rows(order, me, near, far, full):
    size = near.shape[1]
    for i, mask in enumerate(order):
        piece = near[i] if i < near.shape[0] else far[i - near.shape[0]]
        start = pl.multiple_of((me[0] ^ mask) * size, 8)
        full[pl.ds(start, size), :] = piece.astype(F32)


def split_rows(order, me, full, keep, send):
    size = keep.shape[1]
    for i, mask in enumerate(order):
        start = pl.multiple_of((me[0] ^ mask) * size, 8)
        piece = full[pl.ds(start, size), :]
        if i < keep.shape[0]:
            keep[i] = piece
        else:
            send[i - keep.shape[0]] = piece.astype(send.dtype)


def block_kernel(orders, names, sizes, small, large, me, counts, xs, xl, cs, cl, near, far, *rest):
    ys, yl, ds, dl, keep, send = rest[:6]
    vec, kern, gv, gk, gb1, w_ref, g_ref = rest[6:13]
    scratch = rest[13:]
    few = dict(zip(names[: sizes[0]], scratch[: sizes[0]]))
    many = dict(zip(names[sizes[0] :], scratch[sizes[0] :]))
    step = pl.program_id(0)
    d = xs.shape[-1]
    small_steps = sizes[1]
    small_shape, large_shape = small, large

    @pl.when(step == 0)
    def _():
        start_scratch(small_shape, few)
        start_scratch(large_shape, many)
        place_rows(orders[0], me, near, far, g_ref)
        w_ref[...] = g_ref[...].astype(BF)
        for ref in (gv, gk, gb1, g_ref):
            ref[...] = jnp.zeros(ref.shape, ref.dtype)
        vec[...] = jnp.transpose(w_ref[:, 12 * d :].astype(F32))[0:32, :]
        for branch in range(2):
            lanes = slice(branch * LANES, (branch + 1) * LANES)
            for a in range(3):
                for c in range(3):
                    row = 9 + (3 * c + a if branch else 3 * a + c)
                    kern[branch, 3 * a + c : 3 * a + c + 1, :] = vec[row : row + 1, lanes]
            kern[branch, 9:10, :] = vec[8:9, lanes]

    def one(s, b, slot, live, x_ref, cot_ref, y_ref, dx_ref):
        @pl.when(slot < live)
        def _():
            image_step(s, b, x_ref, cot_ref, y_ref, dx_ref, w_ref, g_ref, vec, kern, gv, gk, gb1)

        @pl.when(slot >= live)
        def _():
            y_ref[...] = jnp.zeros(y_ref.shape, y_ref.dtype)
            dx_ref[...] = jnp.zeros(dx_ref.shape, dx_ref.dtype)

    @pl.when(step < small_steps)
    def _():
        one(small_shape, few, step, counts[0, 0], xs, cs, ys, ds)

    @pl.when(step >= small_steps)
    def _():
        one(large_shape, many, step - small_steps, counts[0, 1], xl, cl, yl, dl)

    @pl.when(step == pl.num_programs(0) - 1)
    def _():
        rows = []
        for i in range(8):
            rows.append(jnp.sum(gv[i], axis=0, keepdims=True))

        def taps_row(index, branch):
            return jnp.sum(gk[branch, index], axis=0, keepdims=True)

        rows.append(jnp.concatenate([taps_row(9, 0), taps_row(9, 1)], axis=1))
        for a in range(3):
            for c in range(3):
                rows.append(
                    jnp.concatenate([taps_row(3 * a + c, 0), taps_row(3 * c + a, 1)], axis=1)
                )
        for j in range(4):
            rows.append(jnp.sum(gb1[j], axis=0, keepdims=True))
        rows.append(jnp.zeros((LANES - len(rows), d), F32))
        g_ref[:, 12 * d :] = jnp.transpose(jnp.concatenate(rows, axis=0))
        split_rows(orders[1], me, g_ref, keep, send)


def run_block(small_images, large_images, small_cot, large_cot, counts, me, near, far, orders):
    few, small_cells, d = small_images.shape
    many, large_cells, _ = large_images.shape
    small = Shape(math.isqrt(small_cells))
    large = Shape(math.isqrt(large_cells))
    width = near.shape[2]
    blocks, size = near.shape[0], near.shape[1]
    small_scratch = small.scratch(d, 4 * d)
    large_scratch = large.scratch(d, 4 * d)
    names = tuple(small_scratch) + tuple(large_scratch)
    spaces = [
        pltpu.VMEM(shape, dtype)
        for shape, dtype in list(small_scratch.values()) + list(large_scratch.values())
    ]

    def small_at(i):
        return (jnp.minimum(i, few - 1), 0, 0)

    def large_at(i):
        return (jnp.maximum(i - few, 0), 0, 0)

    small_block = pl.BlockSpec((1, small_cells, d), small_at)
    large_block = pl.BlockSpec((1, large_cells, d), large_at)
    whole = pl.BlockSpec((blocks, size, width), lambda i: (0, 0, 0), pipeline_mode=pl.Buffered(1))
    return pl.pallas_call(
        functools.partial(block_kernel, orders, names, (len(small_scratch), few), small, large),
        grid=(few + many,),
        in_specs=[
            pl.BlockSpec(memory_space=pltpu.SMEM),
            pl.BlockSpec(memory_space=pltpu.SMEM),
            small_block,
            large_block,
            small_block,
            large_block,
            whole,
            whole,
        ],
        out_specs=[small_block, large_block, small_block, large_block, whole, whole],
        out_shape=[
            jax.ShapeDtypeStruct(small_images.shape, BF),
            jax.ShapeDtypeStruct(large_images.shape, BF),
            jax.ShapeDtypeStruct(small_images.shape, F32),
            jax.ShapeDtypeStruct(large_images.shape, F32),
            jax.ShapeDtypeStruct((blocks, size, width), F32),
            jax.ShapeDtypeStruct((blocks, size, width), F32),
        ],
        scratch_shapes=[
            pltpu.VMEM((32, d), F32),
            pltpu.VMEM((2, 16, LANES), F32),
            pltpu.VMEM((8, 8, d), F32),
            pltpu.VMEM((2, 16, 8, LANES), F32),
            pltpu.VMEM((4, 8, d), F32),
            pltpu.VMEM((d, width), BF),
            pltpu.VMEM((d, width), F32),
        ]
        + spaces,
        compiler_params=pltpu.CompilerParams(
            dimension_semantics=("arbitrary",), vmem_limit_bytes=60 * 2**20
        ),
    )(me, counts, small_images, large_images, small_cot, large_cot, near, far)


AXES = ("dp", "fsdp")
ROWS = 8
GROUPS = ((2, 4, 6), (1, 16, 17), (8,))


def gather_order():
    order = [0]
    for group in GROUPS:
        order = order + [o ^ m for m in group for o in order]
    return order


def scatter_order():
    order = [0]
    for group in GROUPS:
        order = [o ^ m for o in (0, *group) for m in order]
    return order


def swap(value, mask, count):
    return lax.ppermute(value, AXES, [(i, i ^ mask) for i in range(count)])


def pack_kernel(*refs):
    out = refs[-1]
    place = 0
    for ref in refs[:-1]:
        width = ref.shape[1]
        out[:, place : place + width] = ref[...].astype(BF)
        place += width
    out[:, place:] = jnp.zeros((out.shape[0], out.shape[1] - place), BF)


def sum_kernel(own, *refs):
    parts, shard, squares = refs[:-2], refs[-2], refs[-1]
    total = own[...]
    for part in parts:
        total = total + part[...].astype(F32)
    shard[...] = total
    square = total * total
    lanes = square[:, 0:LANES]
    for j in range(LANES, square.shape[1], LANES):
        lanes = lanes + square[:, j : j + LANES]
    squares[...] = lanes


def update_kernel(widths, shard, own_squares, far_squares, *refs):
    state, outs = refs[: 3 * len(widths)], refs[3 * len(widths) :]
    both = own_squares[...] + far_squares[...]
    total = jnp.sqrt(jnp.sum(jnp.sum(both, axis=0, keepdims=True), axis=1, keepdims=True))
    clip_factor = jnp.minimum(1.0, clip_norm / (total + 1e-06))
    outs[-1][...] = total
    place = 0
    for i, width in enumerate(widths):
        master, first, second = (ref[...] for ref in state[3 * i : 3 * i + 3])
        gradient = shard[:, place : place + width] * clip_factor
        place += width
        rate, decay = (rate_vector, 0.0) if i == 4 else (rate_matrix, decay_matrix)
        new, first, second = adamw_update(master, first, second, gradient, rate, decay)
        for out, value in zip(outs[4 * i : 4 * i + 4], (new, first, second, new)):
            out[...] = value.astype(out.dtype)


def adamw_update(weight, first, second, gradient, rate, decay):
    first = beta_one * first + (1.0 - beta_one) * gradient
    second = beta_two * second + (1.0 - beta_two) * gradient * gradient
    first_hat = first / (1.0 - beta_one**STEP)
    second_hat = second / (1.0 - beta_two**STEP)
    weight = weight - rate * (first_hat / (jnp.sqrt(second_hat) + adam_epsilon) + decay * weight)
    return (weight, first, second)


def gather_rows(packed, count):
    held = packed[None]
    for group in GROUPS[:-1]:
        held = jnp.concatenate([held] + [swap(held, m, count) for m in group], axis=0)
    return held, swap(held, GROUPS[-1][0], count)


def scatter_rows(keep, send, count):
    held = keep + swap(send, GROUPS[-1][0], count).astype(F32)
    for group in GROUPS[-2::-1]:
        parts = len(group) + 1
        size = held.shape[0] // parts
        pieces = [held[i * size : (i + 1) * size] for i in range(parts)]
        arrived = [swap(p.astype(BF), m, count) for p, m in zip(pieces[1:], group)]
        if group is GROUPS[0]:
            return pieces[0][0], [a[0] for a in arrived]
        held = pieces[0]
        for a in arrived:
            held = held + a.astype(F32)


def on_device(small_images, large_images, small_cot, large_cot, counts, *state):
    d = small_images.shape[-1]
    count = d // state[0].shape[0]
    turned = (False, True, False, True, True)
    state = [v.T if turned[i // 3] else v for i, v in enumerate(state)]
    masters = state[0::3]
    widths = tuple(m.shape[1] for m in masters)
    size = masters[0].shape[0]
    width = sum(widths[:4]) + LANES
    packed = pl.pallas_call(
        pack_kernel, out_shape=jax.ShapeDtypeStruct((size, width), BF)
    )(*masters)
    by_pairs = size == ROWS and (lax.axis_size("dp"), lax.axis_size("fsdp")) == (4, 8)
    if by_pairs:
        near, far = gather_rows(packed, count)
        me = lax.axis_index("dp") * lax.axis_size("fsdp") + lax.axis_index("fsdp")
        orders = (gather_order(), scatter_order())
    else:
        whole = lax.all_gather(packed, AXES, axis=0, tiled=True).reshape(2, -1, ROWS, width)
        near, far = whole[0], whole[1]
        me = jnp.int32(0)
        orders = (range(d // ROWS), range(d // ROWS))
    small_out, large_out, small_back, large_back, keep, send = run_block(
        small_images,
        large_images,
        small_cot,
        large_cot,
        counts,
        me.astype(jnp.int32).reshape(1),
        near,
        far,
        orders,
    )
    if by_pairs:
        own, arrived = scatter_rows(keep, send, count)
    else:
        whole = jnp.concatenate([keep, send], axis=0).reshape(d, width)
        own = lax.psum_scatter(whole, AXES, scatter_dimension=0, tiled=True)
        arrived = []
    shard, squares = pl.pallas_call(
        sum_kernel,
        out_shape=[
            jax.ShapeDtypeStruct((size, width), F32),
            jax.ShapeDtypeStruct((size, LANES), F32),
        ],
    )(own, *arrived)
    if by_pairs:
        for group in GROUPS[:-1]:
            other = [swap(squares, m, count) for m in group]
            squares = (squares + other[0]) + (other[1] + other[2])
        far_squares = swap(squares, GROUPS[-1][0], count)
    else:
        squares = lax.psum(squares, AXES)
        far_squares = jnp.zeros_like(squares)
    new_shapes = []
    for m in masters:
        new_shapes += [jax.ShapeDtypeStruct(m.shape, F32)] * 3 + [jax.ShapeDtypeStruct(m.shape, BF)]
    updated = pl.pallas_call(
        functools.partial(update_kernel, widths),
        out_shape=new_shapes + [jax.ShapeDtypeStruct((1, 1), F32)],
    )(shard, squares, far_squares, *state)
    outs = [v.T if turned[i // 4] else v for i, v in enumerate(updated[:-1])]
    return (small_out, large_out, small_back, large_back, *outs, updated[-1][0, 0])


def solution(mesh):
    cells = P(AXES, None, None)
    rows = P(AXES, None)
    columns = P(None, AXES)
    weights = [rows, columns, rows, columns, columns]
    return jax.shard_map(
        on_device,
        mesh=mesh,
        in_specs=(cells,) * 4 + (rows,) + tuple(w for w in weights for _ in range(3)),
        out_specs=(cells,) * 4 + tuple(w for w in weights for _ in range(4)) + (P(),),
        check_vma=False,
    )
```

```python
import functools
import math

import jax
import jax.numpy as jnp
from jax import lax
from jax.experimental import pallas as pl
from jax.experimental.pallas import tpu as pltpu
from jax.sharding import PartitionSpec as P

HEADS = 8
STRIPE = 7
STEP = 10
LANES = 128

epsilon = 1e-05
clip_norm = 1.0
beta_one = 0.5
beta_two = 0.5
rate_matrix = 0.1
rate_vector = 0.5
decay_matrix = 0.05
adam_epsilon = 1e-08

BF = jnp.bfloat16
F32 = jnp.float32
FAR = -1e30
LOG2E = 1.0 / math.log(2.0)


def dot_nn(a, b):
    return lax.dot_general(a, b, (((1,), (0,)), ((), ())), preferred_element_type=F32)


def dot_nt(a, b):
    return lax.dot_general(a, b, (((1,), (1,)), ((), ())), preferred_element_type=F32)


def dot_tn(a, b):
    return lax.dot_general(a, b, (((0,), (0,)), ((), ())), preferred_element_type=F32)


def fold_rows(v):
    return jnp.sum(v.reshape(v.shape[0] // 8, 8, v.shape[1]), axis=0)


def row_mean(v):
    return jnp.sum(v, axis=-1, keepdims=True) * (1.0 / v.shape[-1])


def gelu_parts(u):
    phi = 0.5 * lax.erf(u * math.sqrt(0.5)) + 0.5
    root = u * math.sqrt(0.5 * LOG2E)
    bell = jnp.exp2(math.log2(1.0 / math.sqrt(2.0 * math.pi)) - root * root)
    return u * phi, phi + u * bell


def shift_down(v, n):
    return jnp.concatenate([jnp.zeros((n, v.shape[1]), v.dtype), v[:-n]], axis=0)


def shift_up(v, n):
    return jnp.concatenate([v[n:], jnp.zeros((n, v.shape[1]), v.dtype)], axis=0)


class Shape:
    def __init__(self, side):
        self.side = side
        self.wide = -(-side // 16) * 16
        self.stripes = side // STRIPE
        self.rows = STRIPE * self.wide
        self.queries = -(-self.rows // LANES) * LANES
        self.all = side * self.wide
        self.deep = -(-self.all // LANES) * LANES
        self.square = self.wide * self.wide

    def scratch(self, d, ff):
        s = self
        both = 2 * s.stripes
        return {
            "raw": ((s.side * s.side, d), F32),
            "x": ((s.all, d), F32),
            "gy": ((s.all, d), F32),
            "n1": ((s.all, d), F32),
            "r1": ((s.all, LANES), F32),
            "out": ((s.all, d), F32),
            "dx1": ((s.all, d), F32),
            "tq": ((3, s.square, LANES), F32),
            "o": ((s.all + s.square, LANES), F32),
            "dq": ((3, s.all + s.square, LANES), F32),
            "q": ((both, s.queries, 2 * LANES), BF),
            "k": ((both, s.queries, 2 * LANES), BF),
            "v": ((both, s.queries, LANES), BF),
            "da": ((both, s.queries, LANES), BF),
            "p": ((both, HEADS // 2, s.queries, s.queries), BF),
            "ot": ((both, LANES, s.queries), F32),
            "ds": ((2, HEADS // 2, s.queries, s.queries), BF),
            "h1": ((s.deep, d), BF),
            "a": ((s.deep, d), BF),
            "h2": ((s.deep, d), BF),
            "gyb": ((s.deep, d), BF),
            "e1": ((s.deep, d), BF),
            "z": ((s.deep, ff), BF),
            "du": ((s.deep, ff), BF),
            "dqkv": ((s.deep, 3 * d), BF),
        }


def head_masks(width):
    lane = lax.broadcasted_iota(jnp.int32, (1, width), 1)
    e = LANES // (HEADS // 2)
    return [
        jnp.where((lane // e == h) | (lane == LANES), 1.0, 0.0).astype(BF)
        for h in range(HEADS // 2)
    ]


def pick_heads(parts):
    e = LANES // (HEADS // 2)
    lane = lax.broadcasted_iota(jnp.int32, parts[0].shape, 1)
    out = parts[-1]
    for h in range(len(parts) - 2, -1, -1):
        out = jnp.where(lane < (h + 1) * e, parts[h], out)
    return out


def place_mask(s, width):
    row = lax.broadcasted_iota(jnp.int32, (s.rows, width), 0)
    return lax.rem(row, s.wide) < s.side


def start_scratch(s, b):
    for name in ("x", "gy"):
        b[name][...] = jnp.zeros(b[name].shape, F32)
    tail = jnp.zeros((s.square - s.all, LANES), F32)
    for which in range(3):
        b["tq"][which, s.all :, :] = tail
        b["dq"][which, 2 * s.all :, :] = tail
    b["o"][2 * s.all :, :] = tail
    extra = s.queries - s.rows
    for sb in range(2 * s.stripes):
        for name in ("q", "k", "v", "da"):
            b[name][sb, s.rows :, :] = jnp.zeros((extra, b[name].shape[2]), BF)
        for h in range(HEADS // 2):
            b["p"][sb, h, s.rows :, :] = jnp.zeros((extra, s.queries), BF)
    for i in range(2):
        for h in range(HEADS // 2):
            b["ds"][i, h, s.rows :, :] = jnp.zeros((extra, s.queries), BF)
    for name in ("h1", "a", "h2", "gyb", "e1", "z", "du", "dqkv"):
        if s.deep > s.all:
            tail = (s.deep - s.all, b[name].shape[1])
            b[name][s.all :, :] = jnp.zeros(tail, BF)
    lane = lax.broadcasted_iota(jnp.int32, (s.rows, LANES), 1)
    one = jnp.where(lane == 0, 1.0, 0.0)
    far = jnp.where((lane == 0) & ~place_mask(s, LANES), FAR, 0.0)
    for sb in range(2 * s.stripes):
        b["q"][sb, 0 : s.rows, LANES:] = one.astype(BF)
        b["k"][sb, 0 : s.rows, LANES:] = far.astype(BF)


def conv_rows(v, taps, s, flip):
    before = pltpu.roll(v, 1, 0)
    after = pltpu.roll(v, v.shape[0] - 1, 0)
    sides = (after, v, before) if flip else (before, v, after)
    mixed = []
    for a in range(3):
        mixed.append(sides[0] * taps[a][0] + sides[1] * taps[a][1] + sides[2] * taps[a][2])
    if flip:
        return mixed[1] + shift_down(mixed[2], s.wide) + shift_up(mixed[0], s.wide)
    return mixed[1] + shift_down(mixed[0], s.wide) + shift_up(mixed[2], s.wide)


def take_turns(*makers):
    running = [m for m in makers if m is not None]
    while running:
        for m in list(running):
            if next(m, running) is running:
                running.remove(m)


def image_step(s, b, x_ref, cot_ref, y_ref, dx_ref, w_ref, g_ref, vec, kern, gv, gk, gb1):
    d = x_ref.shape[-1]
    ff = 4 * d
    heads = HEADS // 2
    e = LANES // heads
    scale = e**-0.5
    o_qkv, o_proj, o_fc1, o_fc2 = 0, 3 * d, 4 * d, 4 * d + ff
    mask = place_mask(s, LANES)

    def rows_of(t):
        return slice(t * s.rows, (t + 1) * s.rows)

    for src, dst in ((x_ref, "x"), (cot_ref, "gy")):
        b["raw"][...] = src[0].astype(F32)
        for r in range(s.side):
            b[dst][r * s.wide : r * s.wide + s.side, :] = b["raw"][
                r * s.side : (r + 1) * s.side, :
            ]

    def phase_a(t):
        rows = rows_of(t)
        x = b["x"][rows, :]
        centered = x - row_mean(x)
        inverse = lax.rsqrt(row_mean(centered * centered) + epsilon)
        n1 = centered * inverse
        b["n1"][rows, :] = n1
        b["r1"][rows, :] = jnp.broadcast_to(inverse, (s.rows, LANES))
        h1 = (n1 * vec[0:1, :] + vec[1:2, :]).astype(BF)
        b["h1"][rows, :] = h1
        joint = dot_nn(h1, w_ref[:, o_qkv : o_qkv + 3 * d])
        q = joint[:, 0:d] + vec[2:3, :]
        k = joint[:, d : 2 * d]
        v = joint[:, 2 * d :] + vec[3:4, :]
        b["q"][t, 0 : s.rows, 0:LANES] = q[:, 0:LANES].astype(BF)
        b["k"][t, 0 : s.rows, 0:LANES] = k[:, 0:LANES].astype(BF)
        b["v"][t, 0 : s.rows, :] = jnp.where(mask, v[:, 0:LANES], 0.0).astype(BF)
        b["tq"][0, rows, :] = q[:, LANES:]
        b["tq"][1, rows, :] = k[:, LANES:]
        b["tq"][2, rows, :] = v[:, LANES:]

    for t in range(s.stripes):
        phase_a(t)

    def turned(cells):
        grid = cells.reshape(s.wide, s.wide, LANES)
        return jnp.swapaxes(grid, 0, 1)[0 : s.side].reshape(s.all, LANES)

    for which, name in enumerate(("q", "k", "v")):
        piece = turned(b["tq"][which])
        for t in range(s.stripes):
            part = piece[t * s.rows : (t + 1) * s.rows]
            b[name][s.stripes + t, 0 : s.rows, 0:LANES] = part.astype(BF)

    def taps_of(branch):
        rows9 = kern[branch]
        return [[rows9[3 * a + c : 3 * a + c + 1, :] for c in range(3)] for a in range(3)], rows9[
            9:10, :
        ]

    masks_wide = head_masks(2 * LANES)
    masks_one = head_masks(LANES)

    def phase_b(sb):
        q = b["q"][sb]
        k = b["k"][sb, 0 : s.rows, :]
        k4 = jnp.concatenate([k * m for m in masks_wide], axis=0)
        s4 = dot_nt(k4, q)
        v = b["v"][sb].astype(F32)
        vt = jnp.transpose(v).astype(BF)
        parts = []
        for h in range(heads):
            sh = s4[h * s.rows : (h + 1) * s.rows, :]
            top = jnp.max(sh, axis=0, keepdims=True)
            ex = jnp.exp2((sh - top) * (scale * LOG2E))
            total = jnp.sum(ex, axis=0, keepdims=True)
            b["p"][sb, h, 0 : s.rows, :] = (ex * (1.0 / total)).astype(BF)
            parts.append(dot_nn(vt[h * e : (h + 1) * e, :], b["p"][sb, h]))
            yield
        ot = jnp.concatenate(parts, axis=0)
        b["ot"][sb] = ot
        o = jnp.transpose(ot)[0 : s.rows, :]
        taps, offset = taps_of(sb // s.stripes)
        pos = conv_rows(v[0 : s.rows, :], taps, s, False) + offset
        b["o"][rows_of(sb), :] = o + pos

    for sb in range(2 * s.stripes):
        take_turns(phase_b(sb))

    b["a"][0 : s.all, LANES:] = turned(b["o"][s.all :, :]).astype(BF)

    def phase_c(t):
        rows = rows_of(t)
        b["a"][rows, 0:LANES] = b["o"][rows, :].astype(BF)
        x1 = b["x"][rows, :] + dot_nt(b["a"][rows, :], w_ref[:, o_proj : o_proj + d]) + vec[4:5, :]
        centered = x1 - row_mean(x1)
        inverse = lax.rsqrt(row_mean(centered * centered) + epsilon)
        n2 = centered * inverse
        h2 = (n2 * vec[5:6, :] + vec[6:7, :]).astype(BF)
        b["h2"][rows, :] = h2
        gy = b["gy"][rows, :]
        gyb = gy.astype(BF)
        b["gyb"][rows, :] = gyb
        out = x1 + vec[7:8, :]
        for j in range(4):
            c1 = slice(o_fc1 + j * d, o_fc1 + (j + 1) * d)
            c2 = slice(o_fc2 + j * d, o_fc2 + (j + 1) * d)
            cj = slice(j * d, (j + 1) * d)
            u = dot_nn(h2, w_ref[:, c1]) + vec[18 + j : 19 + j, :]
            z, slope = gelu_parts(u)
            z = z.astype(BF)
            b["z"][rows, cj] = z
            du = dot_nn(gyb, w_ref[:, c2]) * slope
            gb1[j] += fold_rows(du)
            du = du.astype(BF)
            b["du"][rows, cj] = du
            yield
        out = out + dot_nt(b["z"][rows, :], w_ref[:, o_fc2 : o_fc2 + ff])
        dh2 = dot_nt(b["du"][rows, :], w_ref[:, o_fc1 : o_fc1 + ff])
        b["out"][rows, :] = out
        dn = dh2 * vec[5:6, :]
        dx1 = gy + inverse * (dn - row_mean(dn) - n2 * row_mean(dn * n2))
        b["dx1"][rows, :] = dx1
        e1 = dx1.astype(BF)
        b["e1"][rows, :] = e1
        gv[5] += fold_rows(dh2 * n2)
        gv[6] += fold_rows(dh2)
        gv[7] += fold_rows(gy)
        gv[4] += fold_rows(e1.astype(F32))
        da = dot_nn(e1, w_ref[:, o_proj : o_proj + d])
        b["da"][t, 0 : s.rows, :] = da[:, 0:LANES].astype(BF)
        b["tq"][0, rows, :] = da[:, LANES:]

    def phase_d(sb):
        branch = sb // s.stripes
        v = b["v"][sb, 0 : s.rows, :]
        da = b["da"][sb]
        v4 = jnp.concatenate([v * m for m in masks_one], axis=0)
        dp4 = dot_nt(v4, da)
        mixed = jnp.transpose(da.astype(F32)) * b["ot"][sb]
        kt = jnp.transpose(b["k"][sb, :, 0:LANES].astype(F32)).astype(BF)
        parts = []
        for h in range(heads):
            ph = b["p"][sb, h, 0 : s.rows, :].astype(F32)
            inner = jnp.sum(mixed[h * e : (h + 1) * e, :], axis=0, keepdims=True)
            dp = dp4[h * s.rows : (h + 1) * s.rows, :]
            b["ds"][sb % 2, h, 0 : s.rows, :] = (ph * (dp - inner)).astype(BF)
            parts.append(dot_nn(kt[h * e : (h + 1) * e, :], b["ds"][sb % 2, h]))
            yield
        dq = jnp.transpose(jnp.concatenate(parts, axis=0))[0 : s.rows, :] * scale
        ds4 = jnp.concatenate([b["ds"][sb % 2, h, 0 : s.rows, :] for h in range(heads)], axis=1)
        p4 = jnp.concatenate([b["p"][sb, h, 0 : s.rows, :] for h in range(heads)], axis=1)
        q = b["q"][sb, :, 0:LANES]
        dk = dot_nn(ds4, jnp.concatenate([q * m for m in masks_one], axis=0)) * scale
        dv = dot_nn(p4, jnp.concatenate([da * m for m in masks_one], axis=0))
        taps, offset = taps_of(branch)
        dac = da[0 : s.rows, :].astype(F32)
        vf = v.astype(F32)
        dv = jnp.where(mask, dv + conv_rows(dac, taps, s, True), 0.0)
        rows = rows_of(sb)
        b["dq"][0, rows, :] = dq
        b["dq"][1, rows, :] = dk
        b["dq"][2, rows, :] = dv
        sides = (pltpu.roll(vf, 1, 0), vf, pltpu.roll(vf, s.rows - 1, 0))
        for c in range(3):
            gk[branch, c] += fold_rows(dac[s.wide :] * sides[c][: -s.wide])
            gk[branch, 3 + c] += fold_rows(dac * sides[c])
            gk[branch, 6 + c] += fold_rows(dac[: -s.wide] * sides[c][s.wide :])
        gk[branch, 9] += fold_rows(dac)

    for t in range(s.stripes + 1):
        take_turns(
            phase_c(t) if t < s.stripes else None, phase_d(t - 1) if t > 0 else None
        )

    for r in range(s.side):
        b["raw"][r * s.side : (r + 1) * s.side, :] = b["out"][
            r * s.wide : r * s.wide + s.side, :
        ]
    y_ref[0] = b["raw"][...].astype(BF)

    piece = turned(b["tq"][0])
    for t in range(s.stripes):
        b["da"][s.stripes + t, 0 : s.rows, :] = piece[t * s.rows : (t + 1) * s.rows].astype(BF)

    products = [("h2", "du", o_fc1, j) for j in range(4)]
    products += [("gyb", "z", o_fc2, j) for j in range(4)] + [("e1", "a", o_proj, 0)]
    for sb in range(s.stripes, 2 * s.stripes):
        take_turns(phase_d(sb))
        share = -(-len(products) // (2 * s.stripes - sb))
        for left, right, start, j in products[:share]:
            cj = slice(j * d, (j + 1) * d)
            g_ref[:, start + j * d : start + (j + 1) * d] += dot_tn(
                b[left][...], b[right][:, cj]
            )
        products = products[share:]

    for which in range(3):
        lanes = slice(which * d + LANES, (which + 1) * d)
        b["dqkv"][0 : s.all, lanes] = turned(b["dq"][which, s.all :, :]).astype(BF)

    def phase_e(t):
        rows = rows_of(t)
        for which in range(3):
            b["dqkv"][rows, which * d : which * d + LANES] = b["dq"][which, rows, :].astype(BF)
        dqkv = b["dqkv"][rows, :]
        gv[2] += fold_rows(dqkv[:, 0:d].astype(F32))
        gv[3] += fold_rows(dqkv[:, 2 * d :].astype(F32))
        dh1 = dot_nt(dqkv, w_ref[:, o_qkv : o_qkv + 3 * d])
        n1 = b["n1"][rows, :]
        r1 = b["r1"][rows, :]
        dn = dh1 * vec[0:1, :]
        back = dn - row_mean(dn) - n1 * row_mean(dn * n1)
        b["out"][rows, :] = b["dx1"][rows, :] + back * jnp.concatenate([r1, r1], axis=1)
        gv[0] += fold_rows(dh1 * n1)
        gv[1] += fold_rows(dh1)

    for t in range(s.stripes):
        phase_e(t)

    for r in range(s.side):
        dx_ref[0, r * s.side : (r + 1) * s.side, :] = b["out"][
            r * s.wide : r * s.wide + s.side, :
        ]

    for j in range(0, 3 * d, d):
        g_ref[:, o_qkv + j : o_qkv + j + d] += dot_tn(b["h1"][...], b["dqkv"][:, j : j + d])


def place_rows(order, me, near, far, full):
    size = near.shape[1]
    for i, mask in enumerate(order):
        piece = near[i] if i < near.shape[0] else far[i - near.shape[0]]
        start = pl.multiple_of((me[0] ^ mask) * size, 8)
        full[pl.ds(start, size), :] = piece.astype(F32)


def split_rows(order, me, full, keep, send):
    size = keep.shape[1]
    for i, mask in enumerate(order):
        start = pl.multiple_of((me[0] ^ mask) * size, 8)
        piece = full[pl.ds(start, size), :]
        if i < keep.shape[0]:
            keep[i] = piece
        else:
            send[i - keep.shape[0]] = piece.astype(send.dtype)


def block_kernel(orders, names, sizes, small, large, me, counts, xs, xl, cs, cl, near, far, *rest):
    ys, yl, ds, dl, keep, send = rest[:6]
    vec, kern, gv, gk, gb1, w_ref, g_ref = rest[6:13]
    scratch = rest[13:]
    few = dict(zip(names[: sizes[0]], scratch[: sizes[0]]))
    many = dict(zip(names[sizes[0] :], scratch[sizes[0] :]))
    step = pl.program_id(0)
    d = xs.shape[-1]
    small_steps = sizes[1]
    small_shape, large_shape = small, large

    @pl.when(step == 0)
    def _():
        start_scratch(small_shape, few)
        start_scratch(large_shape, many)
        place_rows(orders[0], me, near, far, g_ref)
        w_ref[...] = g_ref[...].astype(BF)
        for ref in (gv, gk, gb1, g_ref):
            ref[...] = jnp.zeros(ref.shape, ref.dtype)
        vec[...] = jnp.transpose(w_ref[:, 12 * d :].astype(F32))[0:32, :]
        for branch in range(2):
            lanes = slice(branch * LANES, (branch + 1) * LANES)
            for a in range(3):
                for c in range(3):
                    row = 9 + (3 * c + a if branch else 3 * a + c)
                    kern[branch, 3 * a + c : 3 * a + c + 1, :] = vec[row : row + 1, lanes]
            kern[branch, 9:10, :] = vec[8:9, lanes]

    def one(s, b, slot, live, x_ref, cot_ref, y_ref, dx_ref):
        @pl.when(slot < live)
        def _():
            image_step(s, b, x_ref, cot_ref, y_ref, dx_ref, w_ref, g_ref, vec, kern, gv, gk, gb1)

        @pl.when(slot >= live)
        def _():
            y_ref[...] = jnp.zeros(y_ref.shape, y_ref.dtype)
            dx_ref[...] = jnp.zeros(dx_ref.shape, dx_ref.dtype)

    @pl.when(step < small_steps)
    def _():
        one(small_shape, few, step, counts[0, 0], xs, cs, ys, ds)

    @pl.when(step >= small_steps)
    def _():
        one(large_shape, many, step - small_steps, counts[0, 1], xl, cl, yl, dl)

    @pl.when(step == pl.num_programs(0) - 1)
    def _():
        rows = []
        for i in range(8):
            rows.append(jnp.sum(gv[i], axis=0, keepdims=True))

        def taps_row(index, branch):
            return jnp.sum(gk[branch, index], axis=0, keepdims=True)

        rows.append(jnp.concatenate([taps_row(9, 0), taps_row(9, 1)], axis=1))
        for a in range(3):
            for c in range(3):
                rows.append(
                    jnp.concatenate([taps_row(3 * a + c, 0), taps_row(3 * c + a, 1)], axis=1)
                )
        for j in range(4):
            rows.append(jnp.sum(gb1[j], axis=0, keepdims=True))
        rows.append(jnp.zeros((LANES - len(rows), d), F32))
        g_ref[:, 12 * d :] = jnp.transpose(jnp.concatenate(rows, axis=0))
        split_rows(orders[1], me, g_ref, keep, send)


def run_block(small_images, large_images, small_cot, large_cot, counts, me, near, far, orders):
    few, small_cells, d = small_images.shape
    many, large_cells, _ = large_images.shape
    small = Shape(math.isqrt(small_cells))
    large = Shape(math.isqrt(large_cells))
    width = near.shape[2]
    blocks, size = near.shape[0], near.shape[1]
    small_scratch = small.scratch(d, 4 * d)
    large_scratch = large.scratch(d, 4 * d)
    names = tuple(small_scratch) + tuple(large_scratch)
    spaces = [
        pltpu.VMEM(shape, dtype)
        for shape, dtype in list(small_scratch.values()) + list(large_scratch.values())
    ]

    def small_at(i):
        return (jnp.minimum(i, few - 1), 0, 0)

    def large_at(i):
        return (jnp.maximum(i - few, 0), 0, 0)

    small_block = pl.BlockSpec((1, small_cells, d), small_at)
    large_block = pl.BlockSpec((1, large_cells, d), large_at)
    whole = pl.BlockSpec((blocks, size, width), lambda i: (0, 0, 0), pipeline_mode=pl.Buffered(1))
    return pl.pallas_call(
        functools.partial(block_kernel, orders, names, (len(small_scratch), few), small, large),
        grid=(few + many,),
        in_specs=[
            pl.BlockSpec(memory_space=pltpu.SMEM),
            pl.BlockSpec(memory_space=pltpu.SMEM),
            small_block,
            large_block,
            small_block,
            large_block,
            whole,
            whole,
        ],
        out_specs=[small_block, large_block, small_block, large_block, whole, whole],
        out_shape=[
            jax.ShapeDtypeStruct(small_images.shape, BF),
            jax.ShapeDtypeStruct(large_images.shape, BF),
            jax.ShapeDtypeStruct(small_images.shape, F32),
            jax.ShapeDtypeStruct(large_images.shape, F32),
            jax.ShapeDtypeStruct((blocks, size, width), F32),
            jax.ShapeDtypeStruct((blocks, size, width), F32),
        ],
        scratch_shapes=[
            pltpu.VMEM((32, d), F32),
            pltpu.VMEM((2, 16, LANES), F32),
            pltpu.VMEM((8, 8, d), F32),
            pltpu.VMEM((2, 16, 8, LANES), F32),
            pltpu.VMEM((4, 8, d), F32),
            pltpu.VMEM((d, width), BF),
            pltpu.VMEM((d, width), F32),
        ]
        + spaces,
        compiler_params=pltpu.CompilerParams(
            dimension_semantics=("arbitrary",), vmem_limit_bytes=60 * 2**20
        ),
    )(me, counts, small_images, large_images, small_cot, large_cot, near, far)


AXES = ("dp", "fsdp")
ROWS = 8
GROUPS = ((2, 4, 6), (1, 16, 17), (8,))


def gather_order():
    order = [0]
    for group in GROUPS:
        order = order + [o ^ m for m in group for o in order]
    return order


def scatter_order():
    order = [0]
    for group in GROUPS:
        order = [o ^ m for o in (0, *group) for m in order]
    return order


def swap(value, mask, count):
    return lax.ppermute(value, AXES, [(i, i ^ mask) for i in range(count)])


def pack_kernel(*refs):
    out = refs[-1]
    place = 0
    for ref in refs[:-1]:
        width = ref.shape[1]
        out[:, place : place + width] = ref[...].astype(BF)
        place += width
    out[:, place:] = jnp.zeros((out.shape[0], out.shape[1] - place), BF)


def sum_kernel(own, *refs):
    parts, shard, squares = refs[:-2], refs[-2], refs[-1]
    total = own[...]
    for part in parts:
        total = total + part[...].astype(F32)
    shard[...] = total
    square = total * total
    lanes = square[:, 0:LANES]
    for j in range(LANES, square.shape[1], LANES):
        lanes = lanes + square[:, j : j + LANES]
    squares[...] = lanes


def update_kernel(widths, shard, own_squares, far_squares, *refs):
    state, outs = refs[: 3 * len(widths)], refs[3 * len(widths) :]
    both = own_squares[...] + far_squares[...]
    total = jnp.sqrt(jnp.sum(jnp.sum(both, axis=0, keepdims=True), axis=1, keepdims=True))
    clip_factor = jnp.minimum(1.0, clip_norm / (total + 1e-06))
    outs[-1][...] = total
    place = 0
    for i, width in enumerate(widths):
        master, first, second = (ref[...] for ref in state[3 * i : 3 * i + 3])
        gradient = shard[:, place : place + width] * clip_factor
        place += width
        rate, decay = (rate_vector, 0.0) if i == 4 else (rate_matrix, decay_matrix)
        new, first, second = adamw_update(master, first, second, gradient, rate, decay)
        for out, value in zip(outs[4 * i : 4 * i + 4], (new, first, second, new)):
            out[...] = value.astype(out.dtype)


def adamw_update(weight, first, second, gradient, rate, decay):
    first = beta_one * first + (1.0 - beta_one) * gradient
    second = beta_two * second + (1.0 - beta_two) * gradient * gradient
    first_hat = first / (1.0 - beta_one**STEP)
    second_hat = second / (1.0 - beta_two**STEP)
    weight = weight - rate * (first_hat / (jnp.sqrt(second_hat) + adam_epsilon) + decay * weight)
    return (weight, first, second)


def gather_rows(packed, count):
    held = packed[None]
    for group in GROUPS[:-1]:
        held = jnp.concatenate([held] + [swap(held, m, count) for m in group], axis=0)
    return held, swap(held, GROUPS[-1][0], count)


def scatter_rows(keep, send, count):
    held = keep + swap(send, GROUPS[-1][0], count).astype(F32)
    for group in GROUPS[-2::-1]:
        parts = len(group) + 1
        size = held.shape[0] // parts
        pieces = [held[i * size : (i + 1) * size] for i in range(parts)]
        arrived = [swap(p.astype(BF), m, count) for p, m in zip(pieces[1:], group)]
        if group is GROUPS[0]:
            return pieces[0][0], [a[0] for a in arrived]
        held = pieces[0]
        for a in arrived:
            held = held + a.astype(F32)


def on_device(small_images, large_images, small_cot, large_cot, counts, *state):
    d = small_images.shape[-1]
    count = d // state[0].shape[0]
    turned = (False, True, False, True, True)
    state = [v.T if turned[i // 3] else v for i, v in enumerate(state)]
    masters = state[0::3]
    widths = tuple(m.shape[1] for m in masters)
    size = masters[0].shape[0]
    width = sum(widths[:4]) + LANES
    packed = pl.pallas_call(
        pack_kernel, out_shape=jax.ShapeDtypeStruct((size, width), BF)
    )(*masters)
    by_pairs = size == ROWS and (lax.axis_size("dp"), lax.axis_size("fsdp")) == (4, 8)
    if by_pairs:
        near, far = gather_rows(packed, count)
        me = lax.axis_index("dp") * lax.axis_size("fsdp") + lax.axis_index("fsdp")
        orders = (gather_order(), scatter_order())
    else:
        whole = lax.all_gather(packed, AXES, axis=0, tiled=True).reshape(2, -1, ROWS, width)
        near, far = whole[0], whole[1]
        me = jnp.int32(0)
        orders = (range(d // ROWS), range(d // ROWS))
    small_out, large_out, small_back, large_back, keep, send = run_block(
        small_images,
        large_images,
        small_cot,
        large_cot,
        counts,
        me.astype(jnp.int32).reshape(1),
        near,
        far,
        orders,
    )
    if by_pairs:
        own, arrived = scatter_rows(keep, send, count)
    else:
        whole = jnp.concatenate([keep, send], axis=0).reshape(d, width)
        own = lax.psum_scatter(whole, AXES, scatter_dimension=0, tiled=True)
        arrived = []
    shard, squares = pl.pallas_call(
        sum_kernel,
        out_shape=[
            jax.ShapeDtypeStruct((size, width), F32),
            jax.ShapeDtypeStruct((size, LANES), F32),
        ],
    )(own, *arrived)
    if by_pairs:
        for group in GROUPS[:-1]:
            other = [swap(squares, m, count) for m in group]
            squares = (squares + other[0]) + (other[1] + other[2])
        far_squares = swap(squares, GROUPS[-1][0], count)
    else:
        squares = lax.psum(squares, AXES)
        far_squares = jnp.zeros_like(squares)
    new_shapes = []
    for m in masters:
        new_shapes += [jax.ShapeDtypeStruct(m.shape, F32)] * 3 + [jax.ShapeDtypeStruct(m.shape, BF)]
    updated = pl.pallas_call(
        functools.partial(update_kernel, widths),
        out_shape=new_shapes + [jax.ShapeDtypeStruct((1, 1), F32)],
    )(shard, squares, far_squares, *state)
    outs = [v.T if turned[i // 4] else v for i, v in enumerate(updated[:-1])]
    return (small_out, large_out, small_back, large_back, *outs, updated[-1][0, 0])


def solution(mesh):
    cells = P(AXES, None, None)
    rows = P(AXES, None)
    columns = P(None, AXES)
    weights = [rows, columns, rows, columns, columns]
    return jax.shard_map(
        on_device,
        mesh=mesh,
        in_specs=(cells,) * 4 + (rows,) + tuple(w for w in weights for _ in range(3)),
        out_specs=(cells,) * 4 + tuple(w for w in weights for _ in range(4)) + (P(),),
        check_vma=False,
    )
```

```python
import functools
import math

import jax
import jax.numpy as jnp
from jax import lax
from jax.experimental import pallas as pl
from jax.experimental.pallas import tpu as pltpu
from jax.sharding import PartitionSpec as P

HEADS = 8
STRIPE = 7
STEP = 10
LANES = 128

epsilon = 1e-05
clip_norm = 1.0
beta_one = 0.5
beta_two = 0.5
rate_matrix = 0.1
rate_vector = 0.5
decay_matrix = 0.05
adam_epsilon = 1e-08

BF = jnp.bfloat16
F32 = jnp.float32
FAR = -1e30
LOG2E = 1.0 / math.log(2.0)


def dot_nn(a, b):
    return lax.dot_general(a, b, (((1,), (0,)), ((), ())), preferred_element_type=F32)


def dot_nt(a, b):
    return lax.dot_general(a, b, (((1,), (1,)), ((), ())), preferred_element_type=F32)


def dot_tn(a, b):
    return lax.dot_general(a, b, (((0,), (0,)), ((), ())), preferred_element_type=F32)


def fold_rows(v):
    return jnp.sum(v.reshape(v.shape[0] // 8, 8, v.shape[1]), axis=0)


def row_mean(v):
    return jnp.sum(v, axis=-1, keepdims=True) * (1.0 / v.shape[-1])


def gelu_parts(u):
    phi = 0.5 * lax.erf(u * math.sqrt(0.5)) + 0.5
    root = u * math.sqrt(0.5 * LOG2E)
    bell = jnp.exp2(math.log2(1.0 / math.sqrt(2.0 * math.pi)) - root * root)
    return u * phi, phi + u * bell


def shift_down(v, n):
    return jnp.concatenate([jnp.zeros((n, v.shape[1]), v.dtype), v[:-n]], axis=0)


def shift_up(v, n):
    return jnp.concatenate([v[n:], jnp.zeros((n, v.shape[1]), v.dtype)], axis=0)


class Shape:
    def __init__(self, side):
        self.side = side
        self.wide = -(-side // 16) * 16
        self.stripes = side // STRIPE
        self.rows = STRIPE * self.wide
        self.queries = -(-self.rows // LANES) * LANES
        self.all = side * self.wide
        self.deep = -(-self.all // LANES) * LANES
        self.square = self.wide * self.wide

    def scratch(self, d, ff):
        s = self
        both = 2 * s.stripes
        return {
            "raw": ((s.side * s.side, d), F32),
            "x": ((s.all, d), F32),
            "gy": ((s.all, d), F32),
            "n1": ((s.all, d), F32),
            "r1": ((s.all, LANES), F32),
            "out": ((s.all, d), F32),
            "dx1": ((s.all, d), F32),
            "tq": ((3, s.square, LANES), F32),
            "o": ((s.all + s.square, LANES), F32),
            "dq": ((3, s.all + s.square, LANES), F32),
            "q": ((both, s.queries, 2 * LANES), BF),
            "k": ((both, s.queries, 2 * LANES), BF),
            "v": ((both, s.queries, LANES), BF),
            "da": ((both, s.queries, LANES), BF),
            "p": ((both, HEADS // 2, s.queries, s.queries), BF),
            "ot": ((both, LANES, s.queries), F32),
            "ds": ((2, HEADS // 2, s.queries, s.queries), BF),
            "h1": ((s.deep, d), BF),
            "a": ((s.deep, d), BF),
            "h2": ((s.deep, d), BF),
            "gyb": ((s.deep, d), BF),
            "e1": ((s.deep, d), BF),
            "z": ((s.deep, ff), BF),
            "du": ((s.deep, ff), BF),
            "dqkv": ((s.deep, 3 * d), BF),
        }


def head_masks(width):
    lane = lax.broadcasted_iota(jnp.int32, (1, width), 1)
    e = LANES // (HEADS // 2)
    return [
        jnp.where((lane // e == h) | (lane == LANES), 1.0, 0.0).astype(BF)
        for h in range(HEADS // 2)
    ]


def pick_heads(parts):
    e = LANES // (HEADS // 2)
    lane = lax.broadcasted_iota(jnp.int32, parts[0].shape, 1)
    out = parts[-1]
    for h in range(len(parts) - 2, -1, -1):
        out = jnp.where(lane < (h + 1) * e, parts[h], out)
    return out


def place_mask(s, width):
    row = lax.broadcasted_iota(jnp.int32, (s.rows, width), 0)
    return lax.rem(row, s.wide) < s.side


def start_scratch(s, b):
    for name in ("x", "gy"):
        b[name][...] = jnp.zeros(b[name].shape, F32)
    tail = jnp.zeros((s.square - s.all, LANES), F32)
    for which in range(3):
        b["tq"][which, s.all :, :] = tail
        b["dq"][which, 2 * s.all :, :] = tail
    b["o"][2 * s.all :, :] = tail
    extra = s.queries - s.rows
    for sb in range(2 * s.stripes):
        for name in ("q", "k", "v", "da"):
            b[name][sb, s.rows :, :] = jnp.zeros((extra, b[name].shape[2]), BF)
        for h in range(HEADS // 2):
            b["p"][sb, h, s.rows :, :] = jnp.zeros((extra, s.queries), BF)
    for i in range(2):
        for h in range(HEADS // 2):
            b["ds"][i, h, s.rows :, :] = jnp.zeros((extra, s.queries), BF)
    for name in ("h1", "a", "h2", "gyb", "e1", "z", "du", "dqkv"):
        if s.deep > s.all:
            tail = (s.deep - s.all, b[name].shape[1])
            b[name][s.all :, :] = jnp.zeros(tail, BF)
    lane = lax.broadcasted_iota(jnp.int32, (s.rows, LANES), 1)
    one = jnp.where(lane == 0, 1.0, 0.0)
    far = jnp.where((lane == 0) & ~place_mask(s, LANES), FAR, 0.0)
    for sb in range(2 * s.stripes):
        b["q"][sb, 0 : s.rows, LANES:] = one.astype(BF)
        b["k"][sb, 0 : s.rows, LANES:] = far.astype(BF)


def conv_rows(v, taps, s, flip):
    before = pltpu.roll(v, 1, 0)
    after = pltpu.roll(v, v.shape[0] - 1, 0)
    sides = (after, v, before) if flip else (before, v, after)
    mixed = []
    for a in range(3):
        mixed.append(sides[0] * taps[a][0] + sides[1] * taps[a][1] + sides[2] * taps[a][2])
    if flip:
        return mixed[1] + shift_down(mixed[2], s.wide) + shift_up(mixed[0], s.wide)
    return mixed[1] + shift_down(mixed[0], s.wide) + shift_up(mixed[2], s.wide)


def take_turns(*makers):
    running = [m for m in makers if m is not None]
    while running:
        for m in list(running):
            if next(m, running) is running:
                running.remove(m)


def image_step(s, b, x_ref, cot_ref, y_ref, dx_ref, w_ref, g_ref, vec, kern, gv, gk, gb1):
    d = x_ref.shape[-1]
    ff = 4 * d
    heads = HEADS // 2
    e = LANES // heads
    scale = e**-0.5
    o_qkv, o_proj, o_fc1, o_fc2 = 0, 3 * d, 4 * d, 4 * d + ff
    mask = place_mask(s, LANES)

    def rows_of(t):
        return slice(t * s.rows, (t + 1) * s.rows)

    for src, dst in ((x_ref, "x"), (cot_ref, "gy")):
        b["raw"][...] = src[0].astype(F32)
        for r in range(s.side):
            b[dst][r * s.wide : r * s.wide + s.side, :] = b["raw"][
                r * s.side : (r + 1) * s.side, :
            ]

    def phase_a(t):
        rows = rows_of(t)
        x = b["x"][rows, :]
        centered = x - row_mean(x)
        inverse = lax.rsqrt(row_mean(centered * centered) + epsilon)
        n1 = centered * inverse
        b["n1"][rows, :] = n1
        b["r1"][rows, :] = jnp.broadcast_to(inverse, (s.rows, LANES))
        h1 = (n1 * vec[0:1, :] + vec[1:2, :]).astype(BF)
        b["h1"][rows, :] = h1
        joint = dot_nn(h1, w_ref[:, o_qkv : o_qkv + 3 * d])
        q = joint[:, 0:d] + vec[2:3, :]
        k = joint[:, d : 2 * d]
        v = joint[:, 2 * d :] + vec[3:4, :]
        b["q"][t, 0 : s.rows, 0:LANES] = q[:, 0:LANES].astype(BF)
        b["k"][t, 0 : s.rows, 0:LANES] = k[:, 0:LANES].astype(BF)
        b["v"][t, 0 : s.rows, :] = jnp.where(mask, v[:, 0:LANES], 0.0).astype(BF)
        b["tq"][0, rows, :] = q[:, LANES:]
        b["tq"][1, rows, :] = k[:, LANES:]
        b["tq"][2, rows, :] = v[:, LANES:]

    for t in range(s.stripes):
        phase_a(t)

    def turned(cells):
        grid = cells.reshape(s.wide, s.wide, LANES)
        return jnp.swapaxes(grid, 0, 1)[0 : s.side].reshape(s.all, LANES)

    for which, name in enumerate(("q", "k", "v")):
        piece = turned(b["tq"][which])
        for t in range(s.stripes):
            part = piece[t * s.rows : (t + 1) * s.rows]
            b[name][s.stripes + t, 0 : s.rows, 0:LANES] = part.astype(BF)

    def taps_of(branch):
        rows9 = kern[branch]
        return [[rows9[3 * a + c : 3 * a + c + 1, :] for c in range(3)] for a in range(3)], rows9[
            9:10, :
        ]

    masks_wide = head_masks(2 * LANES)
    masks_one = head_masks(LANES)

    def scores_of(sb):
        k = b["k"][sb, 0 : s.rows, :]
        k4 = jnp.concatenate([k * m for m in masks_wide], axis=0)
        return dot_nt(k4, b["q"][sb])

    def phase_b(sb, s4):
        v = b["v"][sb].astype(F32)
        vt = jnp.transpose(v).astype(BF)
        parts = []
        for h in range(heads):
            sh = s4[h * s.rows : (h + 1) * s.rows, :]
            top = jnp.max(sh, axis=0, keepdims=True)
            ex = jnp.exp2((sh - top) * (scale * LOG2E))
            total = jnp.sum(ex, axis=0, keepdims=True)
            b["p"][sb, h, 0 : s.rows, :] = (ex * (1.0 / total)).astype(BF)
            parts.append(dot_nn(vt[h * e : (h + 1) * e, :], b["p"][sb, h]))
            yield
        ot = jnp.concatenate(parts, axis=0)
        b["ot"][sb] = ot
        o = jnp.transpose(ot)[0 : s.rows, :]
        taps, offset = taps_of(sb // s.stripes)
        pos = conv_rows(v[0 : s.rows, :], taps, s, False) + offset
        b["o"][rows_of(sb), :] = o + pos

    ready = scores_of(0)
    for sb in range(2 * s.stripes):
        scores = ready
        if sb + 1 < 2 * s.stripes:
            ready = scores_of(sb + 1)
        take_turns(phase_b(sb, scores))

    b["a"][0 : s.all, LANES:] = turned(b["o"][s.all :, :]).astype(BF)

    def middle_of(t):
        rows = rows_of(t)
        b["a"][rows, 0:LANES] = b["o"][rows, :].astype(BF)
        x1 = b["x"][rows, :] + dot_nt(b["a"][rows, :], w_ref[:, o_proj : o_proj + d]) + vec[4:5, :]
        centered = x1 - row_mean(x1)
        inverse = lax.rsqrt(row_mean(centered * centered) + epsilon)
        n2 = centered * inverse
        return x1, inverse, n2

    def phase_c(t, x1, inverse, n2):
        rows = rows_of(t)
        h2 = (n2 * vec[5:6, :] + vec[6:7, :]).astype(BF)
        b["h2"][rows, :] = h2
        gy = b["gy"][rows, :]
        gyb = gy.astype(BF)
        b["gyb"][rows, :] = gyb
        out = x1 + vec[7:8, :]
        for j in range(4):
            c1 = slice(o_fc1 + j * d, o_fc1 + (j + 1) * d)
            c2 = slice(o_fc2 + j * d, o_fc2 + (j + 1) * d)
            cj = slice(j * d, (j + 1) * d)
            u = dot_nn(h2, w_ref[:, c1]) + vec[18 + j : 19 + j, :]
            z, slope = gelu_parts(u)
            z = z.astype(BF)
            b["z"][rows, cj] = z
            du = dot_nn(gyb, w_ref[:, c2]) * slope
            gb1[j] += fold_rows(du)
            du = du.astype(BF)
            b["du"][rows, cj] = du
            yield
        out = out + dot_nt(b["z"][rows, :], w_ref[:, o_fc2 : o_fc2 + ff])
        dh2 = dot_nt(b["du"][rows, :], w_ref[:, o_fc1 : o_fc1 + ff])
        b["out"][rows, :] = out
        dn = dh2 * vec[5:6, :]
        dx1 = gy + inverse * (dn - row_mean(dn) - n2 * row_mean(dn * n2))
        b["dx1"][rows, :] = dx1
        e1 = dx1.astype(BF)
        b["e1"][rows, :] = e1
        gv[5] += fold_rows(dh2 * n2)
        gv[6] += fold_rows(dh2)
        gv[7] += fold_rows(gy)
        gv[4] += fold_rows(e1.astype(F32))
        da = dot_nn(e1, w_ref[:, o_proj : o_proj + d])
        b["da"][t, 0 : s.rows, :] = da[:, 0:LANES].astype(BF)
        b["tq"][0, rows, :] = da[:, LANES:]

    def phase_d(sb):
        branch = sb // s.stripes
        v = b["v"][sb, 0 : s.rows, :]
        da = b["da"][sb]
        v4 = jnp.concatenate([v * m for m in masks_one], axis=0)
        dp4 = dot_nt(v4, da)
        mixed = jnp.transpose(da.astype(F32)) * b["ot"][sb]
        kt = jnp.transpose(b["k"][sb, :, 0:LANES].astype(F32)).astype(BF)
        parts = []
        for h in range(heads):
            ph = b["p"][sb, h, 0 : s.rows, :].astype(F32)
            inner = jnp.sum(mixed[h * e : (h + 1) * e, :], axis=0, keepdims=True)
            dp = dp4[h * s.rows : (h + 1) * s.rows, :]
            b["ds"][sb % 2, h, 0 : s.rows, :] = (ph * (dp - inner)).astype(BF)
            parts.append(dot_nn(kt[h * e : (h + 1) * e, :], b["ds"][sb % 2, h]))
            yield
        dq = jnp.transpose(jnp.concatenate(parts, axis=0))[0 : s.rows, :] * scale
        ds4 = jnp.concatenate([b["ds"][sb % 2, h, 0 : s.rows, :] for h in range(heads)], axis=1)
        p4 = jnp.concatenate([b["p"][sb, h, 0 : s.rows, :] for h in range(heads)], axis=1)
        q = b["q"][sb, :, 0:LANES]
        dk = dot_nn(ds4, jnp.concatenate([q * m for m in masks_one], axis=0)) * scale
        dv = dot_nn(p4, jnp.concatenate([da * m for m in masks_one], axis=0))
        taps, offset = taps_of(branch)
        dac = da[0 : s.rows, :].astype(F32)
        vf = v.astype(F32)
        dv = jnp.where(mask, dv + conv_rows(dac, taps, s, True), 0.0)
        rows = rows_of(sb)
        b["dq"][0, rows, :] = dq
        b["dq"][1, rows, :] = dk
        b["dq"][2, rows, :] = dv
        sides = (pltpu.roll(vf, 1, 0), vf, pltpu.roll(vf, s.rows - 1, 0))
        for c in range(3):
            gk[branch, c] += fold_rows(dac[s.wide :] * sides[c][: -s.wide])
            gk[branch, 3 + c] += fold_rows(dac * sides[c])
            gk[branch, 6 + c] += fold_rows(dac[: -s.wide] * sides[c][s.wide :])
        gk[branch, 9] += fold_rows(dac)

    ahead = middle_of(0)
    for t in range(s.stripes):
        middle = ahead
        if t + 1 < s.stripes:
            ahead = middle_of(t + 1)
        take_turns(phase_c(t, *middle))

    for r in range(s.side):
        b["raw"][r * s.side : (r + 1) * s.side, :] = b["out"][
            r * s.wide : r * s.wide + s.side, :
        ]
    y_ref[0] = b["raw"][...].astype(BF)

    piece = turned(b["tq"][0])
    for t in range(s.stripes):
        b["da"][s.stripes + t, 0 : s.rows, :] = piece[t * s.rows : (t + 1) * s.rows].astype(BF)

    products = [("h2", "du", o_fc1, j) for j in range(4)]
    products += [("gyb", "z", o_fc2, j) for j in range(4)] + [("e1", "a", o_proj, 0)]
    for sb in range(2 * s.stripes):
        take_turns(phase_d(sb))
        share = -(-len(products) // (2 * s.stripes - sb))
        for left, right, start, j in products[:share]:
            cj = slice(j * d, (j + 1) * d)
            g_ref[:, start + j * d : start + (j + 1) * d] += dot_tn(
                b[left][...], b[right][:, cj]
            )
        products = products[share:]

    for which in range(3):
        lanes = slice(which * d + LANES, (which + 1) * d)
        b["dqkv"][0 : s.all, lanes] = turned(b["dq"][which, s.all :, :]).astype(BF)

    def phase_e(t):
        rows = rows_of(t)
        for which in range(3):
            b["dqkv"][rows, which * d : which * d + LANES] = b["dq"][which, rows, :].astype(BF)
        dqkv = b["dqkv"][rows, :]
        gv[2] += fold_rows(dqkv[:, 0:d].astype(F32))
        gv[3] += fold_rows(dqkv[:, 2 * d :].astype(F32))
        dh1 = dot_nt(dqkv, w_ref[:, o_qkv : o_qkv + 3 * d])
        n1 = b["n1"][rows, :]
        r1 = b["r1"][rows, :]
        dn = dh1 * vec[0:1, :]
        back = dn - row_mean(dn) - n1 * row_mean(dn * n1)
        b["out"][rows, :] = b["dx1"][rows, :] + back * jnp.concatenate([r1, r1], axis=1)
        gv[0] += fold_rows(dh1 * n1)
        gv[1] += fold_rows(dh1)

    for t in range(s.stripes):
        phase_e(t)

    for r in range(s.side):
        dx_ref[0, r * s.side : (r + 1) * s.side, :] = b["out"][
            r * s.wide : r * s.wide + s.side, :
        ]

    for j in range(0, 3 * d, d):
        g_ref[:, o_qkv + j : o_qkv + j + d] += dot_tn(b["h1"][...], b["dqkv"][:, j : j + d])


def place_rows(order, me, near, far, full):
    size = near.shape[1]
    for i, mask in enumerate(order):
        piece = near[i] if i < near.shape[0] else far[i - near.shape[0]]
        start = pl.multiple_of((me[0] ^ mask) * size, 8)
        full[pl.ds(start, size), :] = piece.astype(F32)


def split_rows(order, me, full, keep, send):
    size = keep.shape[1]
    for i, mask in enumerate(order):
        start = pl.multiple_of((me[0] ^ mask) * size, 8)
        piece = full[pl.ds(start, size), :]
        if i < keep.shape[0]:
            keep[i] = piece
        else:
            send[i - keep.shape[0]] = piece.astype(send.dtype)


def block_kernel(orders, names, sizes, small, large, me, counts, xs, xl, cs, cl, near, far, *rest):
    ys, yl, ds, dl, keep, send = rest[:6]
    vec, kern, gv, gk, gb1, w_ref, g_ref = rest[6:13]
    scratch = rest[13:]
    few = dict(zip(names[: sizes[0]], scratch[: sizes[0]]))
    many = dict(zip(names[sizes[0] :], scratch[sizes[0] :]))
    step = pl.program_id(0)
    d = xs.shape[-1]
    small_steps = sizes[1]
    small_shape, large_shape = small, large

    @pl.when(step == 0)
    def _():
        start_scratch(small_shape, few)
        start_scratch(large_shape, many)
        place_rows(orders[0], me, near, far, g_ref)
        w_ref[...] = g_ref[...].astype(BF)
        for ref in (gv, gk, gb1, g_ref):
            ref[...] = jnp.zeros(ref.shape, ref.dtype)
        vec[...] = jnp.transpose(w_ref[:, 12 * d :].astype(F32))[0:32, :]
        for branch in range(2):
            lanes = slice(branch * LANES, (branch + 1) * LANES)
            for a in range(3):
                for c in range(3):
                    row = 9 + (3 * c + a if branch else 3 * a + c)
                    kern[branch, 3 * a + c : 3 * a + c + 1, :] = vec[row : row + 1, lanes]
            kern[branch, 9:10, :] = vec[8:9, lanes]

    def one(s, b, slot, live, x_ref, cot_ref, y_ref, dx_ref):
        @pl.when(slot < live)
        def _():
            image_step(s, b, x_ref, cot_ref, y_ref, dx_ref, w_ref, g_ref, vec, kern, gv, gk, gb1)

        @pl.when(slot >= live)
        def _():
            y_ref[...] = jnp.zeros(y_ref.shape, y_ref.dtype)
            dx_ref[...] = jnp.zeros(dx_ref.shape, dx_ref.dtype)

    @pl.when(step < small_steps)
    def _():
        one(small_shape, few, step, counts[0, 0], xs, cs, ys, ds)

    @pl.when(step >= small_steps)
    def _():
        one(large_shape, many, step - small_steps, counts[0, 1], xl, cl, yl, dl)

    @pl.when(step == pl.num_programs(0) - 1)
    def _():
        rows = []
        for i in range(8):
            rows.append(jnp.sum(gv[i], axis=0, keepdims=True))

        def taps_row(index, branch):
            return jnp.sum(gk[branch, index], axis=0, keepdims=True)

        rows.append(jnp.concatenate([taps_row(9, 0), taps_row(9, 1)], axis=1))
        for a in range(3):
            for c in range(3):
                rows.append(
                    jnp.concatenate([taps_row(3 * a + c, 0), taps_row(3 * c + a, 1)], axis=1)
                )
        for j in range(4):
            rows.append(jnp.sum(gb1[j], axis=0, keepdims=True))
        rows.append(jnp.zeros((LANES - len(rows), d), F32))
        g_ref[:, 12 * d :] = jnp.transpose(jnp.concatenate(rows, axis=0))
        split_rows(orders[1], me, g_ref, keep, send)


def run_block(small_images, large_images, small_cot, large_cot, counts, me, near, far, orders):
    few, small_cells, d = small_images.shape
    many, large_cells, _ = large_images.shape
    small = Shape(math.isqrt(small_cells))
    large = Shape(math.isqrt(large_cells))
    width = near.shape[2]
    blocks, size = near.shape[0], near.shape[1]
    small_scratch = small.scratch(d, 4 * d)
    large_scratch = large.scratch(d, 4 * d)
    names = tuple(small_scratch) + tuple(large_scratch)
    spaces = [
        pltpu.VMEM(shape, dtype)
        for shape, dtype in list(small_scratch.values()) + list(large_scratch.values())
    ]

    def small_at(i):
        return (jnp.minimum(i, few - 1), 0, 0)

    def large_at(i):
        return (jnp.maximum(i - few, 0), 0, 0)

    small_block = pl.BlockSpec((1, small_cells, d), small_at)
    large_block = pl.BlockSpec((1, large_cells, d), large_at)
    whole = pl.BlockSpec((blocks, size, width), lambda i: (0, 0, 0), pipeline_mode=pl.Buffered(1))
    return pl.pallas_call(
        functools.partial(block_kernel, orders, names, (len(small_scratch), few), small, large),
        grid=(few + many,),
        in_specs=[
            pl.BlockSpec(memory_space=pltpu.SMEM),
            pl.BlockSpec(memory_space=pltpu.SMEM),
            small_block,
            large_block,
            small_block,
            large_block,
            whole,
            whole,
        ],
        out_specs=[small_block, large_block, small_block, large_block, whole, whole],
        out_shape=[
            jax.ShapeDtypeStruct(small_images.shape, BF),
            jax.ShapeDtypeStruct(large_images.shape, BF),
            jax.ShapeDtypeStruct(small_images.shape, F32),
            jax.ShapeDtypeStruct(large_images.shape, F32),
            jax.ShapeDtypeStruct((blocks, size, width), F32),
            jax.ShapeDtypeStruct((blocks, size, width), F32),
        ],
        scratch_shapes=[
            pltpu.VMEM((32, d), F32),
            pltpu.VMEM((2, 16, LANES), F32),
            pltpu.VMEM((8, 8, d), F32),
            pltpu.VMEM((2, 16, 8, LANES), F32),
            pltpu.VMEM((4, 8, d), F32),
            pltpu.VMEM((d, width), BF),
            pltpu.VMEM((d, width), F32),
        ]
        + spaces,
        compiler_params=pltpu.CompilerParams(
            dimension_semantics=("arbitrary",), vmem_limit_bytes=60 * 2**20
        ),
    )(me, counts, small_images, large_images, small_cot, large_cot, near, far)


AXES = ("dp", "fsdp")
ROWS = 8
GROUPS = ((2, 4, 6), (1, 16, 17), (8,))


def gather_order():
    order = [0]
    for group in GROUPS:
        order = order + [o ^ m for m in group for o in order]
    return order


def scatter_order():
    order = [0]
    for group in GROUPS:
        order = [o ^ m for o in (0, *group) for m in order]
    return order


def swap(value, mask, count):
    return lax.ppermute(value, AXES, [(i, i ^ mask) for i in range(count)])


def pack_kernel(*refs):
    out = refs[-1]
    place = 0
    for ref in refs[:-1]:
        width = ref.shape[1]
        out[:, place : place + width] = ref[...].astype(BF)
        place += width
    out[:, place:] = jnp.zeros((out.shape[0], out.shape[1] - place), BF)


def sum_kernel(own, *refs):
    parts, shard, squares = refs[:-2], refs[-2], refs[-1]
    total = own[...]
    for part in parts:
        total = total + part[...].astype(F32)
    shard[...] = total
    square = total * total
    lanes = square[:, 0:LANES]
    for j in range(LANES, square.shape[1], LANES):
        lanes = lanes + square[:, j : j + LANES]
    squares[...] = lanes


def update_kernel(widths, shard, own_squares, far_squares, *refs):
    state, outs = refs[: 3 * len(widths)], refs[3 * len(widths) :]
    both = own_squares[...] + far_squares[...]
    total = jnp.sqrt(jnp.sum(jnp.sum(both, axis=0, keepdims=True), axis=1, keepdims=True))
    clip_factor = jnp.minimum(1.0, clip_norm / (total + 1e-06))
    outs[-1][...] = total
    place = 0
    for i, width in enumerate(widths):
        master, first, second = (ref[...] for ref in state[3 * i : 3 * i + 3])
        gradient = shard[:, place : place + width] * clip_factor
        place += width
        rate, decay = (rate_vector, 0.0) if i == 4 else (rate_matrix, decay_matrix)
        new, first, second = adamw_update(master, first, second, gradient, rate, decay)
        for out, value in zip(outs[4 * i : 4 * i + 4], (new, first, second, new)):
            out[...] = value.astype(out.dtype)


def adamw_update(weight, first, second, gradient, rate, decay):
    first = beta_one * first + (1.0 - beta_one) * gradient
    second = beta_two * second + (1.0 - beta_two) * gradient * gradient
    first_hat = first / (1.0 - beta_one**STEP)
    second_hat = second / (1.0 - beta_two**STEP)
    weight = weight - rate * (first_hat / (jnp.sqrt(second_hat) + adam_epsilon) + decay * weight)
    return (weight, first, second)


def gather_rows(packed, count):
    held = packed[None]
    for group in GROUPS[:-1]:
        held = jnp.concatenate([held] + [swap(held, m, count) for m in group], axis=0)
    return held, swap(held, GROUPS[-1][0], count)


def scatter_rows(keep, send, count):
    held = keep + swap(send, GROUPS[-1][0], count).astype(F32)
    for group in GROUPS[-2::-1]:
        parts = len(group) + 1
        size = held.shape[0] // parts
        pieces = [held[i * size : (i + 1) * size] for i in range(parts)]
        arrived = [swap(p.astype(BF), m, count) for p, m in zip(pieces[1:], group)]
        if group is GROUPS[0]:
            return pieces[0][0], [a[0] for a in arrived]
        held = pieces[0]
        for a in arrived:
            held = held + a.astype(F32)


def on_device(small_images, large_images, small_cot, large_cot, counts, *state):
    d = small_images.shape[-1]
    count = d // state[0].shape[0]
    turned = (False, True, False, True, True)
    state = [v.T if turned[i // 3] else v for i, v in enumerate(state)]
    masters = state[0::3]
    widths = tuple(m.shape[1] for m in masters)
    size = masters[0].shape[0]
    width = sum(widths[:4]) + LANES
    packed = pl.pallas_call(
        pack_kernel, out_shape=jax.ShapeDtypeStruct((size, width), BF)
    )(*masters)
    by_pairs = size == ROWS and (lax.axis_size("dp"), lax.axis_size("fsdp")) == (4, 8)
    if by_pairs:
        near, far = gather_rows(packed, count)
        me = lax.axis_index("dp") * lax.axis_size("fsdp") + lax.axis_index("fsdp")
        orders = (gather_order(), scatter_order())
    else:
        whole = lax.all_gather(packed, AXES, axis=0, tiled=True).reshape(2, -1, ROWS, width)
        near, far = whole[0], whole[1]
        me = jnp.int32(0)
        orders = (range(d // ROWS), range(d // ROWS))
    small_out, large_out, small_back, large_back, keep, send = run_block(
        small_images,
        large_images,
        small_cot,
        large_cot,
        counts,
        me.astype(jnp.int32).reshape(1),
        near,
        far,
        orders,
    )
    if by_pairs:
        own, arrived = scatter_rows(keep, send, count)
    else:
        whole = jnp.concatenate([keep, send], axis=0).reshape(d, width)
        own = lax.psum_scatter(whole, AXES, scatter_dimension=0, tiled=True)
        arrived = []
    shard, squares = pl.pallas_call(
        sum_kernel,
        out_shape=[
            jax.ShapeDtypeStruct((size, width), F32),
            jax.ShapeDtypeStruct((size, LANES), F32),
        ],
    )(own, *arrived)
    if by_pairs:
        for group in GROUPS[:-1]:
            other = [swap(squares, m, count) for m in group]
            squares = (squares + other[0]) + (other[1] + other[2])
        far_squares = swap(squares, GROUPS[-1][0], count)
    else:
        squares = lax.psum(squares, AXES)
        far_squares = jnp.zeros_like(squares)
    new_shapes = []
    for m in masters:
        new_shapes += [jax.ShapeDtypeStruct(m.shape, F32)] * 3 + [jax.ShapeDtypeStruct(m.shape, BF)]
    updated = pl.pallas_call(
        functools.partial(update_kernel, widths),
        out_shape=new_shapes + [jax.ShapeDtypeStruct((1, 1), F32)],
    )(shard, squares, far_squares, *state)
    outs = [v.T if turned[i // 4] else v for i, v in enumerate(updated[:-1])]
    return (small_out, large_out, small_back, large_back, *outs, updated[-1][0, 0])


def solution(mesh):
    cells = P(AXES, None, None)
    rows = P(AXES, None)
    columns = P(None, AXES)
    weights = [rows, columns, rows, columns, columns]
    return jax.shard_map(
        on_device,
        mesh=mesh,
        in_specs=(cells,) * 4 + (rows,) + tuple(w for w in weights for _ in range(3)),
        out_specs=(cells,) * 4 + tuple(w for w in weights for _ in range(4)) + (P(),),
        check_vma=False,
    )
```

```python
import functools
import math

import jax
import jax.numpy as jnp
from jax import lax
from jax.experimental import pallas as pl
from jax.experimental.pallas import tpu as pltpu
from jax.sharding import PartitionSpec as P

HEADS = 8
STRIPE = 7
STEP = 10
LANES = 128

epsilon = 1e-05
clip_norm = 1.0
beta_one = 0.5
beta_two = 0.5
rate_matrix = 0.1
rate_vector = 0.5
decay_matrix = 0.05
adam_epsilon = 1e-08

BF = jnp.bfloat16
F32 = jnp.float32
FAR = -1e30
LOG2E = 1.0 / math.log(2.0)


def dot_nn(a, b):
    return lax.dot_general(a, b, (((1,), (0,)), ((), ())), preferred_element_type=F32)


def dot_nt(a, b):
    return lax.dot_general(a, b, (((1,), (1,)), ((), ())), preferred_element_type=F32)


def dot_tn(a, b):
    return lax.dot_general(a, b, (((0,), (0,)), ((), ())), preferred_element_type=F32)


def fold_rows(v):
    return jnp.sum(v.reshape(v.shape[0] // 8, 8, v.shape[1]), axis=0)


def row_mean(v):
    return jnp.sum(v, axis=-1, keepdims=True) * (1.0 / v.shape[-1])


def gelu_parts(u):
    phi = 0.5 * lax.erf(u * math.sqrt(0.5)) + 0.5
    root = u * math.sqrt(0.5 * LOG2E)
    bell = jnp.exp2(math.log2(1.0 / math.sqrt(2.0 * math.pi)) - root * root)
    return u * phi, phi + u * bell


def shift_down(v, n):
    return jnp.concatenate([jnp.zeros((n, v.shape[1]), v.dtype), v[:-n]], axis=0)


def shift_up(v, n):
    return jnp.concatenate([v[n:], jnp.zeros((n, v.shape[1]), v.dtype)], axis=0)


class Shape:
    def __init__(self, side):
        self.side = side
        self.wide = -(-side // 16) * 16
        self.stripes = side // STRIPE
        self.rows = STRIPE * self.wide
        self.queries = -(-self.rows // LANES) * LANES
        self.all = side * self.wide
        self.deep = -(-self.all // LANES) * LANES
        self.square = self.wide * self.wide

    def scratch(self, d, ff):
        s = self
        both = 2 * s.stripes
        return {
            "raw": ((s.side * s.side, d), F32),
            "x": ((s.all, d), F32),
            "gy": ((s.all, d), F32),
            "n1": ((s.all, d), F32),
            "r1": ((s.all, LANES), F32),
            "out": ((s.all, d), F32),
            "dx1": ((s.all, d), F32),
            "tq": ((3, s.square, LANES), F32),
            "o": ((s.all + s.square, LANES), F32),
            "dq": ((3, s.all + s.square, LANES), F32),
            "q": ((both, s.queries, 2 * LANES), BF),
            "k": ((both, s.queries, 2 * LANES), BF),
            "v": ((both, s.queries, LANES), BF),
            "da": ((both, s.queries, LANES), BF),
            "p": ((both, HEADS // 2, s.queries, s.queries), BF),
            "ot": ((both, LANES, s.queries), F32),
            "ds": ((2, HEADS // 2, s.queries, s.queries), BF),
            "h1": ((s.deep, d), BF),
            "a": ((s.deep, d), BF),
            "h2": ((s.deep, d), BF),
            "gyb": ((s.deep, d), BF),
            "e1": ((s.deep, d), BF),
            "z": ((s.deep, ff), BF),
            "du": ((s.deep, ff), BF),
            "dqkv": ((s.deep, 3 * d), BF),
        }


def head_masks(width):
    lane = lax.broadcasted_iota(jnp.int32, (1, width), 1)
    e = LANES // (HEADS // 2)
    return [
        jnp.where((lane // e == h) | (lane == LANES), 1.0, 0.0).astype(BF)
        for h in range(HEADS // 2)
    ]


def pick_heads(parts):
    e = LANES // (HEADS // 2)
    lane = lax.broadcasted_iota(jnp.int32, parts[0].shape, 1)
    out = parts[-1]
    for h in range(len(parts) - 2, -1, -1):
        out = jnp.where(lane < (h + 1) * e, parts[h], out)
    return out


def place_mask(s, width):
    row = lax.broadcasted_iota(jnp.int32, (s.rows, width), 0)
    return lax.rem(row, s.wide) < s.side


def start_scratch(s, b):
    for name in ("x", "gy"):
        b[name][...] = jnp.zeros(b[name].shape, F32)
    tail = jnp.zeros((s.square - s.all, LANES), F32)
    for which in range(3):
        b["tq"][which, s.all :, :] = tail
        b["dq"][which, 2 * s.all :, :] = tail
    b["o"][2 * s.all :, :] = tail
    extra = s.queries - s.rows
    for sb in range(2 * s.stripes):
        for name in ("q", "k", "v", "da"):
            b[name][sb, s.rows :, :] = jnp.zeros((extra, b[name].shape[2]), BF)
        for h in range(HEADS // 2):
            b["p"][sb, h, s.rows :, :] = jnp.zeros((extra, s.queries), BF)
    for i in range(2):
        for h in range(HEADS // 2):
            b["ds"][i, h, s.rows :, :] = jnp.zeros((extra, s.queries), BF)
    for name in ("h1", "a", "h2", "gyb", "e1", "z", "du", "dqkv"):
        if s.deep > s.all:
            tail = (s.deep - s.all, b[name].shape[1])
            b[name][s.all :, :] = jnp.zeros(tail, BF)
    lane = lax.broadcasted_iota(jnp.int32, (s.rows, LANES), 1)
    one = jnp.where(lane == 0, 1.0, 0.0)
    far = jnp.where((lane == 0) & ~place_mask(s, LANES), FAR, 0.0)
    for sb in range(2 * s.stripes):
        b["q"][sb, 0 : s.rows, LANES:] = one.astype(BF)
        b["k"][sb, 0 : s.rows, LANES:] = far.astype(BF)


def conv_rows(v, taps, s, flip):
    before = pltpu.roll(v, 1, 0)
    after = pltpu.roll(v, v.shape[0] - 1, 0)
    sides = (after, v, before) if flip else (before, v, after)
    mixed = []
    for a in range(3):
        mixed.append(sides[0] * taps[a][0] + sides[1] * taps[a][1] + sides[2] * taps[a][2])
    if flip:
        return mixed[1] + shift_down(mixed[2], s.wide) + shift_up(mixed[0], s.wide)
    return mixed[1] + shift_down(mixed[0], s.wide) + shift_up(mixed[2], s.wide)


def take_turns(*makers):
    running = [m for m in makers if m is not None]
    while running:
        for m in list(running):
            if next(m, running) is running:
                running.remove(m)


def image_step(s, b, x_ref, cot_ref, y_ref, dx_ref, w_ref, g_ref, vec, kern, gv, gk, gb1):
    d = x_ref.shape[-1]
    ff = 4 * d
    heads = HEADS // 2
    e = LANES // heads
    scale = e**-0.5
    o_qkv, o_proj, o_fc1, o_fc2 = 0, 3 * d, 4 * d, 4 * d + ff
    mask = place_mask(s, LANES)

    def rows_of(t):
        return slice(t * s.rows, (t + 1) * s.rows)

    for src, dst in ((x_ref, "x"), (cot_ref, "gy")):
        b["raw"][...] = src[0].astype(F32)
        for r in range(s.side):
            b[dst][r * s.wide : r * s.wide + s.side, :] = b["raw"][
                r * s.side : (r + 1) * s.side, :
            ]

    def phase_a(t):
        rows = rows_of(t)
        x = b["x"][rows, :]
        centered = x - row_mean(x)
        inverse = lax.rsqrt(row_mean(centered * centered) + epsilon)
        n1 = centered * inverse
        b["n1"][rows, :] = n1
        b["r1"][rows, :] = jnp.broadcast_to(inverse, (s.rows, LANES))
        h1 = (n1 * vec[0:1, :] + vec[1:2, :]).astype(BF)
        b["h1"][rows, :] = h1
        joint = dot_nn(h1, w_ref[:, o_qkv : o_qkv + 3 * d])
        q = joint[:, 0:d] + vec[2:3, :]
        k = joint[:, d : 2 * d]
        v = joint[:, 2 * d :] + vec[3:4, :]
        b["q"][t, 0 : s.rows, 0:LANES] = q[:, 0:LANES].astype(BF)
        b["k"][t, 0 : s.rows, 0:LANES] = k[:, 0:LANES].astype(BF)
        b["v"][t, 0 : s.rows, :] = jnp.where(mask, v[:, 0:LANES], 0.0).astype(BF)
        b["tq"][0, rows, :] = q[:, LANES:]
        b["tq"][1, rows, :] = k[:, LANES:]
        b["tq"][2, rows, :] = v[:, LANES:]

    for t in range(s.stripes):
        phase_a(t)

    def turned(cells):
        grid = cells.reshape(s.wide, s.wide, LANES)
        return jnp.swapaxes(grid, 0, 1)[0 : s.side].reshape(s.all, LANES)

    for which, name in enumerate(("q", "k", "v")):
        piece = turned(b["tq"][which])
        for t in range(s.stripes):
            part = piece[t * s.rows : (t + 1) * s.rows]
            b[name][s.stripes + t, 0 : s.rows, 0:LANES] = part.astype(BF)

    def taps_of(branch):
        rows9 = kern[branch]
        return [[rows9[3 * a + c : 3 * a + c + 1, :] for c in range(3)] for a in range(3)], rows9[
            9:10, :
        ]

    masks_wide = head_masks(2 * LANES)
    masks_one = head_masks(LANES)

    def scores_of(sb):
        k = b["k"][sb, 0 : s.rows, :]
        k4 = jnp.concatenate([k * m for m in masks_wide], axis=0)
        return dot_nt(k4, b["q"][sb])

    def phase_b(sb, s4):
        v = b["v"][sb].astype(F32)
        vt = jnp.transpose(v).astype(BF)
        parts = []
        for h in range(heads):
            sh = s4[h * s.rows : (h + 1) * s.rows, :]
            top = jnp.max(sh, axis=0, keepdims=True)
            ex = jnp.exp2((sh - top) * (scale * LOG2E))
            total = jnp.sum(ex, axis=0, keepdims=True)
            b["p"][sb, h, 0 : s.rows, :] = (ex * (1.0 / total)).astype(BF)
            parts.append(dot_nn(vt[h * e : (h + 1) * e, :], b["p"][sb, h]))
            yield
        ot = jnp.concatenate(parts, axis=0)
        b["ot"][sb] = ot
        o = jnp.transpose(ot)[0 : s.rows, :]
        taps, offset = taps_of(sb // s.stripes)
        pos = conv_rows(v[0 : s.rows, :], taps, s, False) + offset
        b["o"][rows_of(sb), :] = o + pos

    order = [*range(s.stripes, 2 * s.stripes), *range(s.stripes)]
    ready = scores_of(order[0])
    for i, sb in enumerate(order):
        scores = ready
        if i + 1 < len(order):
            ready = scores_of(order[i + 1])
        take_turns(phase_b(sb, scores))

    b["a"][0 : s.all, LANES:] = turned(b["o"][s.all :, :]).astype(BF)

    def middle_of(t):
        rows = rows_of(t)
        b["a"][rows, 0:LANES] = b["o"][rows, :].astype(BF)
        x1 = b["x"][rows, :] + dot_nt(b["a"][rows, :], w_ref[:, o_proj : o_proj + d]) + vec[4:5, :]
        centered = x1 - row_mean(x1)
        inverse = lax.rsqrt(row_mean(centered * centered) + epsilon)
        n2 = centered * inverse
        return x1, inverse, n2

    def phase_c(t, x1, inverse, n2):
        rows = rows_of(t)
        h2 = (n2 * vec[5:6, :] + vec[6:7, :]).astype(BF)
        b["h2"][rows, :] = h2
        gy = b["gy"][rows, :]
        gyb = gy.astype(BF)
        b["gyb"][rows, :] = gyb
        out = x1 + vec[7:8, :]
        for j in range(4):
            c1 = slice(o_fc1 + j * d, o_fc1 + (j + 1) * d)
            c2 = slice(o_fc2 + j * d, o_fc2 + (j + 1) * d)
            cj = slice(j * d, (j + 1) * d)
            u = dot_nn(h2, w_ref[:, c1]) + vec[18 + j : 19 + j, :]
            z, slope = gelu_parts(u)
            z = z.astype(BF)
            b["z"][rows, cj] = z
            du = dot_nn(gyb, w_ref[:, c2]) * slope
            gb1[j] += fold_rows(du)
            du = du.astype(BF)
            b["du"][rows, cj] = du
            yield
        out = out + dot_nt(b["z"][rows, :], w_ref[:, o_fc2 : o_fc2 + ff])
        dh2 = dot_nt(b["du"][rows, :], w_ref[:, o_fc1 : o_fc1 + ff])
        b["out"][rows, :] = out
        dn = dh2 * vec[5:6, :]
        dx1 = gy + inverse * (dn - row_mean(dn) - n2 * row_mean(dn * n2))
        b["dx1"][rows, :] = dx1
        e1 = dx1.astype(BF)
        b["e1"][rows, :] = e1
        gv[5] += fold_rows(dh2 * n2)
        gv[6] += fold_rows(dh2)
        gv[7] += fold_rows(gy)
        gv[4] += fold_rows(e1.astype(F32))
        da = dot_nn(e1, w_ref[:, o_proj : o_proj + d])
        b["da"][t, 0 : s.rows, :] = da[:, 0:LANES].astype(BF)
        b["tq"][0, rows, :] = da[:, LANES:]

    def phase_d(sb):
        branch = sb // s.stripes
        v = b["v"][sb, 0 : s.rows, :]
        da = b["da"][sb]
        v4 = jnp.concatenate([v * m for m in masks_one], axis=0)
        dp4 = dot_nt(v4, da)
        mixed = jnp.transpose(da.astype(F32)) * b["ot"][sb]
        kt = jnp.transpose(b["k"][sb, :, 0:LANES].astype(F32)).astype(BF)
        parts = []
        for h in range(heads):
            ph = b["p"][sb, h, 0 : s.rows, :].astype(F32)
            inner = jnp.sum(mixed[h * e : (h + 1) * e, :], axis=0, keepdims=True)
            dp = dp4[h * s.rows : (h + 1) * s.rows, :]
            b["ds"][sb % 2, h, 0 : s.rows, :] = (ph * (dp - inner)).astype(BF)
            parts.append(dot_nn(kt[h * e : (h + 1) * e, :], b["ds"][sb % 2, h]))
            yield
        dq = jnp.transpose(jnp.concatenate(parts, axis=0))[0 : s.rows, :] * scale
        ds4 = jnp.concatenate([b["ds"][sb % 2, h, 0 : s.rows, :] for h in range(heads)], axis=1)
        p4 = jnp.concatenate([b["p"][sb, h, 0 : s.rows, :] for h in range(heads)], axis=1)
        q = b["q"][sb, :, 0:LANES]
        dk = dot_nn(ds4, jnp.concatenate([q * m for m in masks_one], axis=0)) * scale
        dv = dot_nn(p4, jnp.concatenate([da * m for m in masks_one], axis=0))
        taps, offset = taps_of(branch)
        dac = da[0 : s.rows, :].astype(F32)
        vf = v.astype(F32)
        dv = jnp.where(mask, dv + conv_rows(dac, taps, s, True), 0.0)
        rows = rows_of(sb)
        b["dq"][0, rows, :] = dq
        b["dq"][1, rows, :] = dk
        b["dq"][2, rows, :] = dv
        sides = (pltpu.roll(vf, 1, 0), vf, pltpu.roll(vf, s.rows - 1, 0))
        for c in range(3):
            gk[branch, c] += fold_rows(dac[s.wide :] * sides[c][: -s.wide])
            gk[branch, 3 + c] += fold_rows(dac * sides[c])
            gk[branch, 6 + c] += fold_rows(dac[: -s.wide] * sides[c][s.wide :])
        gk[branch, 9] += fold_rows(dac)

    ahead = middle_of(0)
    for t in range(s.stripes):
        middle = ahead
        if t + 1 < s.stripes:
            ahead = middle_of(t + 1)
        take_turns(phase_c(t, *middle))

    for r in range(s.side):
        b["raw"][r * s.side : (r + 1) * s.side, :] = b["out"][
            r * s.wide : r * s.wide + s.side, :
        ]
    y_ref[0] = b["raw"][...].astype(BF)

    piece = turned(b["tq"][0])
    for t in range(s.stripes):
        b["da"][s.stripes + t, 0 : s.rows, :] = piece[t * s.rows : (t + 1) * s.rows].astype(BF)

    products = [("h2", "du", o_fc1, j) for j in range(4)]
    products += [("gyb", "z", o_fc2, j) for j in range(4)] + [("e1", "a", o_proj, 0)]
    for sb in range(2 * s.stripes):
        take_turns(phase_d(sb))
        share = -(-len(products) // (2 * s.stripes - sb))
        for left, right, start, j in products[:share]:
            cj = slice(j * d, (j + 1) * d)
            g_ref[:, start + j * d : start + (j + 1) * d] += dot_tn(
                b[left][...], b[right][:, cj]
            )
        products = products[share:]

    for which in range(3):
        lanes = slice(which * d + LANES, (which + 1) * d)
        b["dqkv"][0 : s.all, lanes] = turned(b["dq"][which, s.all :, :]).astype(BF)

    def normed_grad(t):
        rows = rows_of(t)
        for which in range(3):
            b["dqkv"][rows, which * d : which * d + LANES] = b["dq"][which, rows, :].astype(BF)
        dqkv = b["dqkv"][rows, :]
        gv[2] += fold_rows(dqkv[:, 0:d].astype(F32))
        gv[3] += fold_rows(dqkv[:, 2 * d :].astype(F32))
        return dot_nt(dqkv, w_ref[:, o_qkv : o_qkv + 3 * d])

    def phase_e(t, dh1):
        rows = rows_of(t)
        n1 = b["n1"][rows, :]
        r1 = b["r1"][rows, :]
        dn = dh1 * vec[0:1, :]
        back = dn - row_mean(dn) - n1 * row_mean(dn * n1)
        b["out"][rows, :] = b["dx1"][rows, :] + back * jnp.concatenate([r1, r1], axis=1)
        gv[0] += fold_rows(dh1 * n1)
        gv[1] += fold_rows(dh1)

    ahead = normed_grad(0)
    for t in range(s.stripes):
        now = ahead
        if t + 1 < s.stripes:
            ahead = normed_grad(t + 1)
        phase_e(t, now)

    for r in range(s.side):
        dx_ref[0, r * s.side : (r + 1) * s.side, :] = b["out"][
            r * s.wide : r * s.wide + s.side, :
        ]

    for j in range(0, 3 * d, d):
        g_ref[:, o_qkv + j : o_qkv + j + d] += dot_tn(b["h1"][...], b["dqkv"][:, j : j + d])


def place_rows(order, me, near, far, full):
    size = near.shape[1]
    for i, mask in enumerate(order):
        piece = near[i] if i < near.shape[0] else far[i - near.shape[0]]
        start = pl.multiple_of((me[0] ^ mask) * size, 8)
        full[pl.ds(start, size), :] = piece.astype(F32)


def split_rows(order, me, full, keep, send):
    size = keep.shape[1]
    for i, mask in enumerate(order):
        start = pl.multiple_of((me[0] ^ mask) * size, 8)
        piece = full[pl.ds(start, size), :]
        if i < keep.shape[0]:
            keep[i] = piece
        else:
            send[i - keep.shape[0]] = piece.astype(send.dtype)


def block_kernel(orders, names, sizes, small, large, me, counts, xs, xl, cs, cl, near, far, *rest):
    ys, yl, ds, dl, keep, send = rest[:6]
    vec, kern, gv, gk, gb1, w_ref, g_ref = rest[6:13]
    scratch = rest[13:]
    few = dict(zip(names[: sizes[0]], scratch[: sizes[0]]))
    many = dict(zip(names[sizes[0] :], scratch[sizes[0] :]))
    step = pl.program_id(0)
    d = xs.shape[-1]
    small_steps = sizes[1]
    small_shape, large_shape = small, large

    @pl.when(step == 0)
    def _():
        start_scratch(small_shape, few)
        start_scratch(large_shape, many)
        place_rows(orders[0], me, near, far, g_ref)
        w_ref[...] = g_ref[...].astype(BF)
        for ref in (gv, gk, gb1, g_ref):
            ref[...] = jnp.zeros(ref.shape, ref.dtype)
        vec[...] = jnp.transpose(w_ref[:, 12 * d :].astype(F32))[0:32, :]
        for branch in range(2):
            lanes = slice(branch * LANES, (branch + 1) * LANES)
            for a in range(3):
                for c in range(3):
                    row = 9 + (3 * c + a if branch else 3 * a + c)
                    kern[branch, 3 * a + c : 3 * a + c + 1, :] = vec[row : row + 1, lanes]
            kern[branch, 9:10, :] = vec[8:9, lanes]

    def one(s, b, slot, live, x_ref, cot_ref, y_ref, dx_ref):
        @pl.when(slot < live)
        def _():
            image_step(s, b, x_ref, cot_ref, y_ref, dx_ref, w_ref, g_ref, vec, kern, gv, gk, gb1)

        @pl.when(slot >= live)
        def _():
            y_ref[...] = jnp.zeros(y_ref.shape, y_ref.dtype)
            dx_ref[...] = jnp.zeros(dx_ref.shape, dx_ref.dtype)

    @pl.when(step < small_steps)
    def _():
        one(small_shape, few, step, counts[0, 0], xs, cs, ys, ds)

    @pl.when(step >= small_steps)
    def _():
        one(large_shape, many, step - small_steps, counts[0, 1], xl, cl, yl, dl)

    @pl.when(step == pl.num_programs(0) - 1)
    def _():
        rows = []
        for i in range(8):
            rows.append(jnp.sum(gv[i], axis=0, keepdims=True))

        def taps_row(index, branch):
            return jnp.sum(gk[branch, index], axis=0, keepdims=True)

        rows.append(jnp.concatenate([taps_row(9, 0), taps_row(9, 1)], axis=1))
        for a in range(3):
            for c in range(3):
                rows.append(
                    jnp.concatenate([taps_row(3 * a + c, 0), taps_row(3 * c + a, 1)], axis=1)
                )
        for j in range(4):
            rows.append(jnp.sum(gb1[j], axis=0, keepdims=True))
        rows.append(jnp.zeros((LANES - len(rows), d), F32))
        g_ref[:, 12 * d :] = jnp.transpose(jnp.concatenate(rows, axis=0))
        split_rows(orders[1], me, g_ref, keep, send)


def run_block(small_images, large_images, small_cot, large_cot, counts, me, near, far, orders):
    few, small_cells, d = small_images.shape
    many, large_cells, _ = large_images.shape
    small = Shape(math.isqrt(small_cells))
    large = Shape(math.isqrt(large_cells))
    width = near.shape[2]
    blocks, size = near.shape[0], near.shape[1]
    small_scratch = small.scratch(d, 4 * d)
    large_scratch = large.scratch(d, 4 * d)
    names = tuple(small_scratch) + tuple(large_scratch)
    spaces = [
        pltpu.VMEM(shape, dtype)
        for shape, dtype in list(small_scratch.values()) + list(large_scratch.values())
    ]

    def small_at(i):
        return (jnp.minimum(i, few - 1), 0, 0)

    def large_at(i):
        return (jnp.maximum(i - few, 0), 0, 0)

    small_block = pl.BlockSpec((1, small_cells, d), small_at)
    large_block = pl.BlockSpec((1, large_cells, d), large_at)
    whole = pl.BlockSpec((blocks, size, width), lambda i: (0, 0, 0), pipeline_mode=pl.Buffered(1))
    return pl.pallas_call(
        functools.partial(block_kernel, orders, names, (len(small_scratch), few), small, large),
        grid=(few + many,),
        in_specs=[
            pl.BlockSpec(memory_space=pltpu.SMEM),
            pl.BlockSpec(memory_space=pltpu.SMEM),
            small_block,
            large_block,
            small_block,
            large_block,
            whole,
            whole,
        ],
        out_specs=[small_block, large_block, small_block, large_block, whole, whole],
        out_shape=[
            jax.ShapeDtypeStruct(small_images.shape, BF),
            jax.ShapeDtypeStruct(large_images.shape, BF),
            jax.ShapeDtypeStruct(small_images.shape, F32),
            jax.ShapeDtypeStruct(large_images.shape, F32),
            jax.ShapeDtypeStruct((blocks, size, width), F32),
            jax.ShapeDtypeStruct((blocks, size, width), F32),
        ],
        scratch_shapes=[
            pltpu.VMEM((32, d), F32),
            pltpu.VMEM((2, 16, LANES), F32),
            pltpu.VMEM((8, 8, d), F32),
            pltpu.VMEM((2, 16, 8, LANES), F32),
            pltpu.VMEM((4, 8, d), F32),
            pltpu.VMEM((d, width), BF),
            pltpu.VMEM((d, width), F32),
        ]
        + spaces,
        compiler_params=pltpu.CompilerParams(
            dimension_semantics=("arbitrary",), vmem_limit_bytes=60 * 2**20
        ),
    )(me, counts, small_images, large_images, small_cot, large_cot, near, far)


AXES = ("dp", "fsdp")
ROWS = 8
GROUPS = ((2, 4, 6), (1, 16, 17), (8,))


def gather_order():
    order = [0]
    for group in GROUPS:
        order = order + [o ^ m for m in group for o in order]
    return order


def scatter_order():
    order = [0]
    for group in GROUPS:
        order = [o ^ m for o in (0, *group) for m in order]
    return order


def swap(value, mask, count):
    return lax.ppermute(value, AXES, [(i, i ^ mask) for i in range(count)])


def pack_kernel(*refs):
    out = refs[-1]
    place = 0
    for ref in refs[:-1]:
        width = ref.shape[1]
        out[:, place : place + width] = ref[...].astype(BF)
        place += width
    out[:, place:] = jnp.zeros((out.shape[0], out.shape[1] - place), BF)


def sum_kernel(own, *refs):
    parts, shard, squares = refs[:-2], refs[-2], refs[-1]
    total = own[...]
    for part in parts:
        total = total + part[...].astype(F32)
    shard[...] = total
    square = total * total
    lanes = square[:, 0:LANES]
    for j in range(LANES, square.shape[1], LANES):
        lanes = lanes + square[:, j : j + LANES]
    squares[...] = lanes


def update_kernel(widths, shard, own_squares, far_squares, *refs):
    state, outs = refs[: 3 * len(widths)], refs[3 * len(widths) :]
    both = own_squares[...] + far_squares[...]
    total = jnp.sqrt(jnp.sum(jnp.sum(both, axis=0, keepdims=True), axis=1, keepdims=True))
    clip_factor = jnp.minimum(1.0, clip_norm / (total + 1e-06))
    outs[-1][...] = total
    place = 0
    for i, width in enumerate(widths):
        master, first, second = (ref[...] for ref in state[3 * i : 3 * i + 3])
        gradient = shard[:, place : place + width] * clip_factor
        place += width
        rate, decay = (rate_vector, 0.0) if i == 4 else (rate_matrix, decay_matrix)
        new, first, second = adamw_update(master, first, second, gradient, rate, decay)
        for out, value in zip(outs[4 * i : 4 * i + 4], (new, first, second, new)):
            out[...] = value.astype(out.dtype)


def adamw_update(weight, first, second, gradient, rate, decay):
    first = beta_one * first + (1.0 - beta_one) * gradient
    second = beta_two * second + (1.0 - beta_two) * gradient * gradient
    first_hat = first / (1.0 - beta_one**STEP)
    second_hat = second / (1.0 - beta_two**STEP)
    weight = weight - rate * (first_hat / (jnp.sqrt(second_hat) + adam_epsilon) + decay * weight)
    return (weight, first, second)


def gather_rows(packed, count):
    held = packed[None]
    for group in GROUPS[:-1]:
        held = jnp.concatenate([held] + [swap(held, m, count) for m in group], axis=0)
    return held, swap(held, GROUPS[-1][0], count)


def scatter_rows(keep, send, count):
    held = keep + swap(send, GROUPS[-1][0], count).astype(F32)
    for group in GROUPS[-2::-1]:
        parts = len(group) + 1
        size = held.shape[0] // parts
        pieces = [held[i * size : (i + 1) * size] for i in range(parts)]
        arrived = [swap(p.astype(BF), m, count) for p, m in zip(pieces[1:], group)]
        if group is GROUPS[0]:
            return pieces[0][0], [a[0] for a in arrived]
        held = pieces[0]
        for a in arrived:
            held = held + a.astype(F32)


def on_device(small_images, large_images, small_cot, large_cot, counts, *state):
    d = small_images.shape[-1]
    count = d // state[0].shape[0]
    turned = (False, True, False, True, True)
    state = [v.T if turned[i // 3] else v for i, v in enumerate(state)]
    masters = state[0::3]
    widths = tuple(m.shape[1] for m in masters)
    size = masters[0].shape[0]
    width = sum(widths[:4]) + LANES
    packed = pl.pallas_call(
        pack_kernel, out_shape=jax.ShapeDtypeStruct((size, width), BF)
    )(*masters)
    by_pairs = size == ROWS and (lax.axis_size("dp"), lax.axis_size("fsdp")) == (4, 8)
    if by_pairs:
        near, far = gather_rows(packed, count)
        me = lax.axis_index("dp") * lax.axis_size("fsdp") + lax.axis_index("fsdp")
        orders = (gather_order(), scatter_order())
    else:
        whole = lax.all_gather(packed, AXES, axis=0, tiled=True).reshape(2, -1, ROWS, width)
        near, far = whole[0], whole[1]
        me = jnp.int32(0)
        orders = (range(d // ROWS), range(d // ROWS))
    small_out, large_out, small_back, large_back, keep, send = run_block(
        small_images,
        large_images,
        small_cot,
        large_cot,
        counts,
        me.astype(jnp.int32).reshape(1),
        near,
        far,
        orders,
    )
    if by_pairs:
        own, arrived = scatter_rows(keep, send, count)
    else:
        whole = jnp.concatenate([keep, send], axis=0).reshape(d, width)
        own = lax.psum_scatter(whole, AXES, scatter_dimension=0, tiled=True)
        arrived = []
    shard, squares = pl.pallas_call(
        sum_kernel,
        out_shape=[
            jax.ShapeDtypeStruct((size, width), F32),
            jax.ShapeDtypeStruct((size, LANES), F32),
        ],
    )(own, *arrived)
    if by_pairs:
        for group in GROUPS[:-1]:
            other = [swap(squares, m, count) for m in group]
            squares = (squares + other[0]) + (other[1] + other[2])
        far_squares = swap(squares, GROUPS[-1][0], count)
    else:
        squares = lax.psum(squares, AXES)
        far_squares = jnp.zeros_like(squares)
    new_shapes = []
    for m in masters:
        new_shapes += [jax.ShapeDtypeStruct(m.shape, F32)] * 3 + [jax.ShapeDtypeStruct(m.shape, BF)]
    updated = pl.pallas_call(
        functools.partial(update_kernel, widths),
        out_shape=new_shapes + [jax.ShapeDtypeStruct((1, 1), F32)],
    )(shard, squares, far_squares, *state)
    outs = [v.T if turned[i // 4] else v for i, v in enumerate(updated[:-1])]
    return (small_out, large_out, small_back, large_back, *outs, updated[-1][0, 0])


def solution(mesh):
    cells = P(AXES, None, None)
    rows = P(AXES, None)
    columns = P(None, AXES)
    weights = [rows, columns, rows, columns, columns]
    return jax.shard_map(
        on_device,
        mesh=mesh,
        in_specs=(cells,) * 4 + (rows,) + tuple(w for w in weights for _ in range(3)),
        out_specs=(cells,) * 4 + tuple(w for w in weights for _ in range(4)) + (P(),),
        check_vma=False,
    )
```
